32 devices in a mesh: group: 2 (over y), dom: 8 (over z, x), feat: 2 (over core).
Axes of the slice: x: 2, y: 2, z: 4, core: 2. Of those that a mesh axis runs over, the one named last changes fastest.
Arguments:
- features: bfloat16 [16384, 128], P(('group', 'dom')), parts along dimension 0, may hold values from -6 to 6
- w_self: bfloat16 [128, 256], P(None, 'feat'), may hold values from -0.5 to 0.5
- w_neigh: bfloat16 [128, 256], P(None, 'feat'), may hold values from -0.5 to 0.5
- bias: float32 [256], P('feat'), may hold values from -3 to 3
- cotangent: bfloat16 [16384, 256], P(('group', 'dom'), 'feat'), parts along dimension 0, may hold values from -6 to 6
- adjacency: bfloat16 [896, 256, 256], P(('group', 'dom')), parts along dimension 0, may hold values from -0.1875 to 0.1875
- tile_dst: int32 [896], P(('group', 'dom')), parts along dimension 0, may hold values from 0 to 3
- tile_src: int32 [896], P(('group', 'dom')), parts along dimension 0, may hold values from 0 to 5
- tile_count: int32 [16], P(('group', 'dom')), parts along dimension 0, may hold values from 1 to 56, 149 in all
- send_rows: int32 [16, 8, 2], P(('group', 'dom')), parts along dimension 0, may hold values from 0 to 1023
- send_count: int32 [16, 8], P(('group', 'dom')), parts along dimension 0, may hold values from 0 to 2, as said below
- hub_owner: int32 [32, 1], P('group'), parts along dimension 0, may hold values from 0 to 7; in each aligned block of 16 rows (0 to 15, 16 to 31, ...) at most 4 rows name the same one
- hub_row: int32 [32], P('group'), parts along dimension 0, may hold values from 0 to 1023
Outputs:
- output: bfloat16 [16384, 256], P(('group', 'dom'), 'feat'), parts along dimension 0
- grad_features: bfloat16 [16384, 128], P(('group', 'dom')), parts along dimension 0
- grad_w_self: float32 [256, 256], P('group', 'feat'), parts along dimension 0
- grad_w_neigh: float32 [256, 256], P('group', 'feat'), parts along dimension 0
- grad_bias: float32 [512], P(('group', 'feat')), parts along dimension 0
The draws below stay inside these ranges and needn't reach their ends.
There are 2 independent parts, one for each index of `group`. The reference program is written for one: setup_inputs(seed, part) draws one part's arguments, and reference() takes and returns one part's arrays. A program takes and returns all parts, laid end to end along the dimension named above; an argument that names none is the same for every part. Nothing has to cross between parts.
Inputs may be any that keep to these rules, and one draw needn't show every extreme that they name: `send_count`: entry [q, p] is how many rows partition q sends to partition p; zero where q equals p; some partition receives 2 rows from every other partition. Only the first send_count[q, p] slots of send_rows[q, p] are sent. `hub_owner`: no partition owns more than 4 hubs, and some partition owns exactly 4. `tile_src`: source blocks 0 to 3 are the partition's own rows, then 1 block of received rows, then 1 block of hub rows. Tiles at position tile_count or later are not part of the graph; some partition uses all 56.
All inputs are finite; a program needn't handle non-finite values. No bound on the sum of `tile_count` on one device may be relied on, other than what follows from the above.
Results may differ from the reference program's by a relative error of at most 0.0058.
Values may be sent and summed in bfloat16 or wider, within the bound.
No kernel may reach another device: no remote copies, remote signals or barrier semaphores. Data moves between devices by JAX's collectives and lax.ppermute only.
A program may use at most 64 MiB of HBM per device.

```python
import math
import jax
import jax.numpy as jnp
import numpy as np
from jax import lax

F_IN = 128
H = 256
TILE = 256
NODE_DEV = 1024
TILE_MAX = 56
SLOT = 2
HUB_MOST = 4
NODES = 8192
HUBS = 16
TILES = 448
DST_BLOCKS = 4
HALO_BLOCKS = 1
HUB_BLOCKS = 1
SRC_BLOCKS = 6
N_DOM = 8


def draw_send_count(key, part):
    key = jax.random.fold_in(key, 7)
    first_key, second_key = jax.random.split(key)
    counts = jax.random.randint(first_key, (N_DOM, N_DOM), 0, SLOT + 1)
    receiver = jax.random.randint(second_key, (), 0, N_DOM)
    column = jnp.arange(N_DOM)[None, :]
    counts = jnp.where(column == receiver, SLOT, counts)
    counts = jnp.where(column == jnp.arange(N_DOM)[:, None], 0, counts)
    return counts.astype(jnp.int32)


def plant(drawn, key, least, largest):
    longest = drawn.shape.index(max(drawn.shape))
    spots = []
    for shift in (0, 1):
        where = [jax.random.randint(jax.random.fold_in(key, axis), (), 0, length) for axis, length in enumerate(drawn.shape)]
        where[longest] = (where[longest] + shift) % drawn.shape[longest]
        spots.append(tuple(where))
    return drawn.at[spots[0]].set(least).at[spots[1]].set(largest)


def block_scale(rng, shape, cuts, smallest, largest):
    loudness = 1.0
    for dim, shards_of in cuts:
        draws = jax.random.uniform(jax.random.fold_in(jax.random.fold_in(rng, 6), dim), (shards_of,), jnp.float32, smallest / len(cuts), largest / len(cuts))
        loudness = loudness * jnp.repeat(jnp.exp(draws), shape[dim] // shards_of).reshape((-1,) + (1,) * (len(shape) - 1 - dim))
    return loudness


def length_profile(count, total, bound, skew):
    portions = [(1 << 20) // math.isqrt(standing ** skew) + 1 for standing in range(2, count + 1)]
    spare, given = total - bound - (count - 1), [1] * (count - 1)
    while spare > 0:
        movable = [i for i in range(count - 1) if given[i] < bound]
        pool, remaining = sum([portions[i] for i in movable]), spare
        for i in movable:
            addition = min(bound - given[i], max(1, remaining * portions[i] // pool), spare)
            given[i] = given[i] + addition
            spare = spare - addition
    return np.array([bound] + given)


def uneven(own_key, amount, total, most, lean):
    if amount == 2:
        one = jax.random.randint(own_key, (), max(1, total - most), min(most, total - 1) + 1)
        return jnp.stack([one, total - one])
    sizes = jnp.asarray(length_profile(amount, total, most, lean), jnp.int32)
    couples = (amount - 1) // 2
    source_of, taker = sizes[1:1 + 2 * couples:2], sizes[2:2 + 2 * couples:2]
    slack = jnp.minimum(source_of - 1, most - taker)
    moved = jax.random.randint(jax.random.fold_in(own_key, 1), (couples,), 0, 1 << 20) % (slack + 1)
    sizes = sizes.at[1:1 + 2 * couples:2].set(source_of - moved).at[2:2 + 2 * couples:2].set(taker + moved)
    return sizes[jax.random.permutation(jax.random.fold_in(own_key, 2), amount)]


def shared_out(own_key, own, number, rows, number_of, top, reach, lean):
    sequence = jax.random.permutation(own_key, number_of)
    crowded, common = portions_of(number_of, rows * top, reach, lean, True), portions_of(number_of, rows * top, reach, lean, False)
    places = jnp.arange(number_of)

    def named(tallies, offset_by):
        used = int((tallies > 0).sum())
        fixed = max(1, used // 4)
        passed = fixed + (places - fixed + offset_by * (used - fixed)) % max(1, number_of - fixed)
        return jnp.zeros((number_of,), jnp.int32).at[sequence[jnp.where(places < fixed, places, passed)]].set(jnp.asarray(tallies, jnp.int32))

    tallies = jnp.where(number % 4 == 0, named(crowded, number // 4), named(common, number - number // 4 - 1))
    mixed = jax.random.permutation(jax.random.fold_in(own, 3), number_of)
    source_of, sink = mixed[0:number_of // 2 * 2:2], mixed[1:number_of // 2 * 2:2]
    margin = jnp.minimum(tallies[source_of] - 1, reach - tallies[sink]) // 2
    margin = jnp.where((source_of == sequence[0]) | (sink == sequence[0]) | (tallies[sink] == 0), 0, jnp.maximum(margin, 0))
    passed = jax.random.randint(jax.random.fold_in(own, 4), (number_of // 2,), 0, 1 << 20) % (margin + 1)
    tallies = tallies.at[source_of].add(-passed).at[sink].add(passed)
    items = jnp.searchsorted(jnp.cumsum(tallies), jnp.arange(rows * top), side="right").astype(jnp.int32)
    listing = items.reshape(top, rows).T
    listing = listing[jax.random.permutation(jax.random.fold_in(own, 1), rows)]
    offset_by = jax.random.randint(jax.random.fold_in(own, 2), (rows, 1), 0, top)
    return jnp.take_along_axis(listing, (jnp.arange(top)[None, :] + offset_by) % top, axis=1)


def portions_of(count, total, most, lean, full):
    portions = [(1 << 20) // math.isqrt(standing ** lean) + 1 for standing in range(1, count + 1)]
    largest = most if full else min(most, max(-(-total // count), total * portions[0] // sum(portions)))
    least = 1 if total - largest >= count - 1 else 0
    given, spare = [largest] + [least] * (count - 1), total - largest - least * (count - 1)
    while spare > 0:
        candidates = [i for i in range(1, count) if given[i] < largest] or [i for i in range(1, count) if given[i] < most]
        whole, remaining = sum([portions[i] for i in candidates]), spare
        for i in candidates:
            extra = min(most - given[i], max(1, remaining * portions[i] // whole), spare)
            given[i] = given[i] + extra
            spare = spare - extra
    return np.array(given)


def gaussian(key, shape, deviation, bound, pieces=(), held_as=jnp.bfloat16):
    entries = deviation * jax.random.normal(key, shape, jnp.float32)
    if pieces:
        entries = entries * block_scale(key, shape, pieces, -0.22, 0.18)
    return jnp.clip(entries, -bound, bound).astype(held_as)


def setup_inputs(seed: int = 0, part: int = 0) -> dict:
    streams_of = jax.random.split(jax.random.key(seed), 14)
    own_keys = jax.random.split(jax.random.fold_in(streams_of[13], part), 14)
    features = gaussian(own_keys[0], (NODES, F_IN), 1.0, 6.0, ((0, 8),))
    w_self = gaussian(streams_of[1], (F_IN, H), F_IN ** -0.5, 0.5, ((1, 2),))
    w_neigh = gaussian(streams_of[2], (F_IN, H), F_IN ** -0.5, 0.5, ((1, 2),))
    bias = gaussian(streams_of[3], (H,), 0.5, 3.0, ((0, 2),), jnp.float32)
    cotangent = gaussian(own_keys[4], (NODES, H), 1.0, 6.0, ((0, 8), (1, 2)))
    adjacency = gaussian(own_keys[5], (TILES, TILE, TILE), (max(1, TILE * TILE_MAX // (3 * DST_BLOCKS))) ** -0.5, 0.1875, ((0, 8),))
    tile_dst = plant(jax.random.randint(own_keys[6], (TILES,), 0, DST_BLOCKS), jax.random.fold_in(own_keys[6], 1), 0, DST_BLOCKS - 1).astype(jnp.int32)
    tile_src = plant(jax.random.randint(own_keys[7], (TILES,), 0, SRC_BLOCKS), jax.random.fold_in(own_keys[7], 1), 0, SRC_BLOCKS - 1).astype(jnp.int32)
    tile_count = uneven(own_keys[8], N_DOM, N_DOM * TILE_MAX // 3, TILE_MAX, 2).astype(jnp.int32)
    send_rows = plant(jax.random.randint(own_keys[9], (N_DOM, N_DOM, SLOT), 0, NODE_DEV), jax.random.fold_in(own_keys[9], 1), 0, NODE_DEV - 1).astype(jnp.int32)
    send_count = draw_send_count(jax.random.fold_in(jax.random.fold_in(streams_of[13], part), 71), part)
    hub_owner_keys = jax.random.split(jax.random.fold_in(own_keys[11], 1), HUBS // HUBS)
    hub_owner_turns = jax.random.permutation(jax.random.fold_in(own_keys[11], 3), HUBS // HUBS)
    hub_owner = jax.vmap(lambda own, number: shared_out(jax.random.fold_in(own_keys[11], 2), own, number, HUBS, N_DOM, 1, HUB_MOST, 2))(hub_owner_keys, hub_owner_turns).reshape((HUBS, 1))
    hub_row = plant(jax.random.randint(own_keys[12], (HUBS,), 0, NODE_DEV), jax.random.fold_in(own_keys[12], 1), 0, NODE_DEV - 1).astype(jnp.int32)
    return {"features": features, "w_self": w_self, "w_neigh": w_neigh, "bias": bias, "cotangent": cotangent, "adjacency": adjacency, "tile_dst": tile_dst, "tile_src": tile_src, "tile_count": tile_count, "send_rows": send_rows, "send_count": send_count, "hub_owner": hub_owner, "hub_row": hub_row}


def activate(values):
    return jax.nn.gelu(values, approximate=True)

def activation_grad(preact, upstream):
    return jax.vjp(activate, preact)[1](upstream)[0]

def reference(features, w_self, w_neigh, bias, cotangent, adjacency, tile_dst, tile_src, tile_count, send_rows, send_count, hub_owner, hub_row):
    hidden_cols = w_neigh.shape[1]
    highest = lax.Precision.HIGHEST
    projected = jnp.dot(features, w_neigh, preferred_element_type=jnp.float32).astype(jnp.bfloat16)
    own_term = jnp.dot(features, w_self, preferred_element_type=jnp.float32)
    node_base = (jnp.arange(N_DOM) * NODE_DEV).astype(jnp.int32)
    halo_index = (jnp.transpose(send_rows, (1, 0, 2)).astype(jnp.int32) + node_base[None, :, None]).reshape(N_DOM, N_DOM * SLOT)
    halo_mask = (jnp.arange(SLOT)[None, None, :] < jnp.transpose(send_count)[:, :, None]).reshape(N_DOM, N_DOM * SLOT)
    halo_extra = HALO_BLOCKS * TILE - N_DOM * SLOT
    halo_index = jnp.concatenate([halo_index, jnp.zeros((N_DOM, halo_extra), jnp.int32)], axis=1)
    halo_mask = jnp.concatenate([halo_mask, jnp.zeros((N_DOM, halo_extra), bool)], axis=1)
    hub_index = (hub_owner[:, 0] * NODE_DEV + hub_row).astype(jnp.int32)
    hub_extra = HUB_BLOCKS * TILE - HUBS
    hub_index = jnp.concatenate([hub_index, jnp.zeros((hub_extra,), jnp.int32)])
    hub_mask = jnp.arange(HUB_BLOCKS * TILE) < HUBS
    local_index = node_base[:, None] + jnp.arange(NODE_DEV).astype(jnp.int32)[None, :]
    source_index = jnp.concatenate([local_index, halo_index, jnp.broadcast_to(hub_index[None, :], (N_DOM, HUB_BLOCKS * TILE))], axis=1).astype(jnp.int32)
    source_mask = jnp.concatenate([jnp.ones((N_DOM, NODE_DEV), bool), halo_mask, jnp.broadcast_to(hub_mask[None, :], (N_DOM, HUB_BLOCKS * TILE))], axis=1).astype(jnp.float32)
    tiles_each = adjacency.reshape(N_DOM, TILE_MAX, TILE, TILE)
    dst_each = tile_dst.reshape(N_DOM, TILE_MAX).astype(jnp.int32)
    src_each = tile_src.reshape(N_DOM, TILE_MAX).astype(jnp.int32)
    in_graph = jnp.arange(TILE_MAX)[None, None, :] < tile_count[:, None, None]
    dst_select = ((dst_each[:, None, :] == jnp.arange(DST_BLOCKS)[None, :, None]) & in_graph).astype(jnp.float32)
    src_select = ((src_each[:, None, :] == jnp.arange(SRC_BLOCKS)[None, :, None]) & in_graph).astype(jnp.float32)

    def gather_side(operands):
        index, mask, tiles, sources, dst_pick = operands
        gathered = (projected[index].astype(jnp.float32) * mask[:, None]).astype(jnp.bfloat16)
        blocks = gathered.reshape(SRC_BLOCKS, TILE, hidden_cols)
        chosen = blocks[sources].astype(jnp.float32)
        products = jnp.einsum('trs,tsi->tri', tiles.astype(jnp.float32), chosen, precision=highest)
        summed = jnp.einsum('dt,tri->dri', dst_pick, products, precision=highest)
        return summed.reshape(NODE_DEV, hidden_cols)
    aggregate = lax.map(gather_side, (source_index, source_mask, tiles_each, src_each, dst_select)).reshape(NODES, hidden_cols)
    preact = own_term + aggregate + bias[None, :]
    output = activate(preact).astype(jnp.bfloat16)
    grad_pre = activation_grad(preact, cotangent.astype(jnp.float32))
    grad_pre_low = grad_pre.astype(jnp.bfloat16)
    grads_each = grad_pre_low.reshape(N_DOM, DST_BLOCKS, TILE, hidden_cols)

    def scatter_side(operands):
        mask, tiles, targets, src_pick, upstream = operands
        picked = upstream[targets].astype(jnp.float32)
        transposed = jnp.einsum('trs,tri->tsi', tiles.astype(jnp.float32), picked, precision=highest)
        summed = jnp.einsum('bt,tsi->bsi', src_pick, transposed, precision=highest)
        return summed.reshape(SRC_BLOCKS * TILE, hidden_cols) * mask[:, None]
    source_grads = lax.map(scatter_side, (source_mask, tiles_each, dst_each, src_select, grads_each))
    grad_proj = jnp.zeros((NODES, hidden_cols), jnp.float32).at[source_index.reshape(-1)].add(source_grads.reshape(-1, hidden_cols))
    grad_proj_low = grad_proj.astype(jnp.bfloat16)
    contract_rows = (((0,), (0,)), ((), ()))
    contract_cols = (((1,), (1,)), ((), ()))
    grad_w_self = lax.dot_general(features, grad_pre_low, contract_rows, preferred_element_type=jnp.float32)
    grad_w_neigh = lax.dot_general(features, grad_proj_low, contract_rows, preferred_element_type=jnp.float32)
    grad_bias = lax.optimization_barrier(jnp.sum(grad_pre, axis=0))
    grad_features = (lax.dot_general(grad_pre_low, w_self, contract_cols, preferred_element_type=jnp.float32) + lax.dot_general(grad_proj_low, w_neigh, contract_cols, preferred_element_type=jnp.float32)).astype(jnp.bfloat16)
    return (output, grad_features, grad_w_self, grad_w_neigh, grad_bias)
```

```python
import functools

import jax
import jax.numpy as jnp
from jax import lax
from jax.experimental import pallas as pl
from jax.experimental.pallas import tpu as pltpu
from jax.sharding import PartitionSpec as P

HUB_MOST = 4
PEER_ROWS = 8
GROUP_TILES = 8
F32 = jnp.float32
BF16 = jnp.bfloat16
NT = (((1,), (1,)), ((), ()))


def dot(a, b):
    return jnp.dot(a, b, preferred_element_type=F32)


def dot_nt(a, b):
    return lax.dot_general(a, b, NT, preferred_element_type=F32)


def repeat(count, body, init):
    return lax.fori_loop(0, count, body, init, unroll=True)


def hub_slots(owner_ref, counter_ref, partitions, body):
    def clear(q, carry):
        counter_ref[q] = 0
        return carry

    def visit(hub, carry):
        owner = owner_ref[hub]
        slot = counter_ref[owner]
        counter_ref[owner] = slot + 1
        body(hub, owner, slot)
        return carry

    repeat(partitions, clear, 0)
    repeat(owner_ref.shape[0], visit, 0)


def fetch(pairs, sems):
    copies = [pltpu.make_async_copy(src, dst, sems.at[k]) for k, (src, dst) in enumerate(pairs)]
    for copy in copies:
        copy.start()
    return copies


def gather_kernel(
    rows_hbm, count_hbm, owner_hbm, hub_row_hbm, features_hbm,
    bundle_ref,
    rows_ref, count_ref, owner_ref, hub_row_ref, features_ref, wide_ref, hubs_ref, sems,
):
    own = lax.axis_index("dom")
    partitions = bundle_ref.shape[0]
    slots = rows_ref.shape[0]
    copies = fetch(
        [
            (features_hbm, features_ref), (rows_hbm, rows_ref), (count_hbm, count_ref),
            (owner_hbm, owner_ref), (hub_row_hbm, hub_row_ref),
        ],
        sems,
    )
    hubs_ref[...] = jnp.zeros_like(hubs_ref)
    for copy in copies:
        copy.wait()
    wide_ref[...] = features_ref[...].astype(F32)

    def hub(index, slot):
        mine = owner_ref[index] == own

        @pl.when(mine)
        def _():
            hubs_ref[pl.ds(slots + slot, 1), :] = wide_ref[pl.ds(hub_row_ref[index], 1), :]

        return slot + mine.astype(jnp.int32)

    repeat(owner_ref.shape[0], hub, jnp.int32(0))

    def peer(q, carry):
        bundle_ref[q] = hubs_ref[...]
        for slot in range(slots):
            row = wide_ref[pl.ds(rows_ref[slot, q], 1), :]
            bundle_ref[q, slot : slot + 1, :] = jnp.where(slot < count_ref[q], row, 0.0)
        return carry

    repeat(partitions, peer, 0)


def put(list_ref, position, tile, dst, src):
    list_ref[0, position] = tile
    list_ref[1, position] = dst
    list_ref[2, position] = src


def split_tiles(near_ref, far_ref, dst_ref, src_ref, count, split):
    def visit(tile, used):
        src, dst = src_ref[tile], dst_ref[tile]
        near, far = used
        put(near_ref, near, tile, dst, src)
        put(far_ref, far, tile, dst, src)
        is_near = (src < split).astype(jnp.int32)
        return near + is_near, far + 1 - is_near

    return lax.fori_loop(0, count, visit, (jnp.int32(0), jnp.int32(0)))


def pad_list(list_ref, used, dst, src):
    first = list_ref[0, 0]
    for k in range(GROUP_TILES):
        put(list_ref, used + k, first, dst, src)


class Tiles:
    def __init__(self, list_ref, total, source, held, sems):
        self.list_ref, self.total, self.source, self.held, self.sems = list_ref, total, source, held, sems

    def copy(self, position):
        tile = self.list_ref[0, position]
        return pltpu.make_async_copy(self.source.at[tile], self.held.at[tile], self.sems.at[tile])

    def start(self):
        def one(position, carry):
            self.copy(position).start()
            return carry

        lax.fori_loop(0, self.total, one, 0)

    def each(self, body, wait):
        def group(step, carry):
            if wait:
                for k in range(GROUP_TILES):
                    position = step * GROUP_TILES + k

                    @pl.when(position < self.total)
                    def _(position=position):
                        self.copy(position).wait()

            for k in range(GROUP_TILES):
                position = step * GROUP_TILES + k
                tile = self.held[self.list_ref[0, position]]
                body(tile, self.list_ref[1, position], self.list_ref[2, position])
            return carry

        lax.fori_loop(0, (self.total + GROUP_TILES - 1) // GROUP_TILES, group, 0)


def own_kernel(
    dst_hbm, src_hbm, count_hbm, features_hbm, w_self_hbm, w_neigh_hbm, bias_hbm, adjacency_hbm,
    total_ref,
    dst_ref, src_ref, count_ref, features_ref, w_self_ref, w_neigh_ref, bias_ref,
    adjacency_ref, blocks_ref, list_ref, far_list_ref, sems, tile_sems,
):
    tile_rows = adjacency_ref.shape[1]
    dst_blocks = total_ref.shape[0] - 1
    copies = fetch(
        [
            (src_hbm, src_ref), (dst_hbm, dst_ref), (count_hbm, count_ref), (w_neigh_hbm, w_neigh_ref),
            (features_hbm, features_ref), (w_self_hbm, w_self_ref), (bias_hbm, bias_ref),
        ],
        sems,
    )
    for copy in copies[:3]:
        copy.wait()
    used, _ = split_tiles(list_ref, far_list_ref, dst_ref, src_ref, count_ref[0], dst_blocks)
    pad_list(list_ref, used, dst_blocks, dst_blocks)
    tiles = Tiles(list_ref, used, adjacency_hbm, adjacency_ref, tile_sems)
    tiles.start()
    for copy in copies[3:]:
        copy.wait()
    features = features_ref[...]
    projected = dot(features, w_neigh_ref[...]).astype(BF16)
    for block in range(dst_blocks):
        blocks_ref[block] = projected[block * tile_rows : (block + 1) * tile_rows]
    blocks_ref[dst_blocks] = jnp.zeros(blocks_ref.shape[1:], BF16)
    base = dot(features, w_self_ref[...]) + bias_ref[...]
    for block in range(dst_blocks):
        total_ref[block] = base[block * tile_rows : (block + 1) * tile_rows]
    total_ref[dst_blocks] = jnp.zeros(total_ref.shape[1:], F32)

    def forward(tile, dst, src):
        total_ref[dst] += dot(tile, blocks_ref[src])

    tiles.each(forward, wait=True)


def rest_kernel(
    dst_ref, src_ref, count_ref, owner_ref,
    arrived_ref, total_hbm, features_ref, w_self_ref, w_neigh_ref, cotangent_ref, adjacency_hbm,
    output_ref, partial_ref, pack_ref,
    total_ref, rows_ref, low_rows_ref, blocks_ref, grad_ref, grad_t_ref, source_t_ref, back_ref,
    adjacency_ref, far_list_ref, own_list_ref, counter_ref, tile_sems, total_sem,
    *, partitions, slots,
):
    tile_rows = adjacency_ref.shape[1]
    dst_blocks = total_hbm.shape[0] - 1
    halo_blocks = -(-partitions * slots // tile_rows)
    hub_blocks = -(-owner_ref.shape[0] // tile_rows)
    extra_blocks = halo_blocks + hub_blocks
    hub_base = halo_blocks * tile_rows
    source_blocks = dst_blocks + extra_blocks
    fetch_total = pltpu.make_async_copy(total_hbm, total_ref, total_sem)
    fetch_total.start()
    near_used, far_used = split_tiles(own_list_ref, far_list_ref, dst_ref, src_ref, count_ref[0], dst_blocks)
    far = Tiles(far_list_ref, far_used, adjacency_hbm, adjacency_ref, tile_sems)
    far.start()
    own = Tiles(own_list_ref, near_used, adjacency_hbm, adjacency_ref, tile_sems)
    own.start()
    pad_list(far_list_ref, far_used, dst_blocks, source_blocks)
    pad_list(own_list_ref, near_used, dst_blocks, source_blocks)

    rows_ref[...] = jnp.zeros_like(rows_ref)

    def halo_in(q, carry):
        rows_ref[pl.ds(q * slots, slots), :] = arrived_ref[q, 0:slots, :]
        return carry

    repeat(partitions, halo_in, 0)

    def hub_in(hub, owner, slot):
        rows_ref[pl.ds(hub_base + hub, 1), :] = arrived_ref[owner, pl.ds(slots + slot, 1), :]

    hub_slots(owner_ref, counter_ref, partitions, hub_in)
    low_rows_ref[...] = rows_ref[...].astype(BF16)
    for block in range(extra_blocks):
        rows = low_rows_ref[block * tile_rows : (block + 1) * tile_rows]
        blocks_ref[block] = dot(rows, w_neigh_ref[...]).astype(BF16)
    blocks_ref[extra_blocks] = jnp.zeros(blocks_ref.shape[1:], BF16)
    fetch_total.wait()

    def forward(tile, dst, src):
        total_ref[dst] += dot(tile, blocks_ref[src - dst_blocks])

    far.each(forward, wait=True)

    root = 0.7978845608028654
    bias_sum = jnp.zeros((1, output_ref.shape[1]), F32)
    w_self_t = jnp.zeros((output_ref.shape[1], features_ref.shape[1]), F32)
    for block in range(dst_blocks):
        span = slice(block * tile_rows, (block + 1) * tile_rows)
        v = total_ref[block]
        square = v * v
        gate = jnp.tanh(root * (v + 0.044715 * (v * square)))
        half = 0.5 * (1.0 + gate)
        output_ref[span, :] = (v * half).astype(BF16)
        slope = half + (0.5 * root) * v * (1.0 - gate * gate) * (1.0 + (3 * 0.044715) * square)
        grad = cotangent_ref[span, :].astype(F32) * slope
        bias_sum += jnp.sum(grad, axis=0, keepdims=True)
        low = grad.astype(BF16)
        grad_ref[block] = low
        low_t = jnp.transpose(grad).astype(BF16)
        grad_t_ref[block] = low_t
        w_self_t += dot(low_t, features_ref[span, :])
    grad_t_ref[dst_blocks] = jnp.zeros(grad_t_ref.shape[1:], BF16)

    source_t_ref[...] = jnp.zeros_like(source_t_ref)

    def backward(tile, dst, src):
        source_t_ref[src] += dot(grad_t_ref[dst], tile)

    far.each(backward, wait=False)
    own.each(backward, wait=True)

    w_neigh_t = jnp.zeros_like(w_self_t)
    for block in range(dst_blocks):
        span = slice(block * tile_rows, (block + 1) * tile_rows)
        source_t = source_t_ref[block]
        w_neigh_t += dot(source_t.astype(BF16), features_ref[span, :])
        partial_ref[span, :] = dot_nt(grad_ref[block], w_self_ref[...]) + dot_nt(
            jnp.transpose(source_t).astype(BF16), w_neigh_ref[...]
        )
    for block in range(extra_blocks):
        span = slice(block * tile_rows, (block + 1) * tile_rows)
        source_t = source_t_ref[dst_blocks + block]
        w_neigh_t += dot(source_t.astype(BF16), low_rows_ref[span, :])
        back_ref[span, :] = dot_nt(jnp.transpose(source_t).astype(BF16), w_neigh_ref[...])

    w_self = jnp.transpose(w_self_t)
    w_neigh = jnp.transpose(w_neigh_t)
    share = w_self.shape[0] // partitions
    for q in range(partitions):
        pack_ref[q, PEER_ROWS : PEER_ROWS + share, :] = w_self[q * share : (q + 1) * share]
        pack_ref[q, PEER_ROWS + share : PEER_ROWS + 2 * share, :] = w_neigh[q * share : (q + 1) * share]

    def halo_out(q, carry):
        pack_ref[q, 0:PEER_ROWS, :] = jnp.zeros((PEER_ROWS, pack_ref.shape[2]), F32)
        pack_ref[q, 0:slots, :] = back_ref[pl.ds(q * slots, slots), :]
        pack_ref[q, PEER_ROWS - 1 : PEER_ROWS, :] = bias_sum
        return carry

    repeat(partitions, halo_out, 0)

    def hub_out(hub, owner, slot):
        pack_ref[owner, pl.ds(slots + slot, 1), :] = back_ref[pl.ds(hub_base + hub, 1), :]

    hub_slots(owner_ref, counter_ref, partitions, hub_out)


def merge_kernel(
    rows_ref, count_ref, owner_ref, hub_row_ref, arrived_ref, partial_ref,
    share_ref, bias_ref, low_ref, total_ref, hubs_ref,
):
    own = lax.axis_index("dom")
    partitions = arrived_ref.shape[0]
    slots = rows_ref.shape[0]
    summed = jnp.sum(arrived_ref[...], axis=0)
    bias_ref[...] = summed[PEER_ROWS - 1 : PEER_ROWS]
    hubs_ref[...] = summed[0:PEER_ROWS]
    shares = summed[PEER_ROWS:]
    for q in range(partitions):
        share_ref[q] = shares
    total_ref[...] = partial_ref[...]

    def peer(q, carry):
        for slot in range(slots):
            row = pl.ds(rows_ref[slot, q], 1)
            total_ref[row, :] += jnp.where(slot < count_ref[q], arrived_ref[q, slot : slot + 1, :], 0.0)
        return carry

    repeat(partitions, peer, 0)

    def hub(index, slot):
        mine = owner_ref[index] == own

        @pl.when(mine)
        def _():
            total_ref[pl.ds(hub_row_ref[index], 1), :] += hubs_ref[pl.ds(slots + slot, 1), :]

        return slot + mine.astype(jnp.int32)

    repeat(owner_ref.shape[0], hub, jnp.int32(0))
    low_ref[...] = total_ref[...].astype(BF16)


SMEM = pl.BlockSpec(memory_space=pltpu.SMEM)
VMEM = pl.BlockSpec(memory_space=pltpu.VMEM)
HBM = pl.BlockSpec(memory_space=pltpu.HBM)


def call(kernel, name, ins, outs, scratch, args, grant, flops=0, size=0):
    return pl.pallas_call(
        kernel,
        out_shape=outs,
        in_specs=ins,
        out_specs=jax.tree.map(lambda _: VMEM, outs),
        scratch_shapes=scratch,
        compiler_params=pltpu.CompilerParams(vmem_limit_bytes=grant * 1024 * 1024),
        cost_estimate=pl.CostEstimate(flops=flops, bytes_accessed=size, transcendentals=0),
        name=name,
    )(*args)


def local(
    features, w_self, w_neigh, bias, cotangent, adjacency, tile_dst, tile_src, tile_count,
    send_rows, send_count, hub_owner, hub_row,
):
    nodes, inputs = features.shape
    limit, tile_rows, _ = adjacency.shape
    hidden = w_neigh.shape[1]
    partitions = lax.axis_size("dom")
    slots = send_rows.shape[2]
    hubs = hub_row.shape[0]
    dst_blocks = nodes // tile_rows
    extra_blocks = -(-partitions * slots // tile_rows) - (-hubs // tile_rows)
    share = inputs // partitions
    rows = jnp.transpose(send_rows[0])
    counts = send_count.reshape(partitions)
    owner = hub_owner.reshape(hubs)
    struct = jax.ShapeDtypeStruct
    lists = pltpu.SMEM((3, limit + GROUP_TILES), jnp.int32)

    bundle = call(
        gather_kernel, "gather", [HBM] * 5,
        struct((partitions, PEER_ROWS, inputs), F32),
        [
            pltpu.SMEM((slots, partitions), jnp.int32),
            pltpu.SMEM((partitions,), jnp.int32),
            pltpu.SMEM((hubs,), jnp.int32),
            pltpu.SMEM((hubs,), jnp.int32),
            pltpu.VMEM((nodes, inputs), BF16),
            pltpu.VMEM((nodes, inputs), F32),
            pltpu.VMEM((PEER_ROWS, inputs), F32),
            pltpu.SemaphoreType.DMA((5,)),
        ],
        (rows, counts, owner, hub_row, features), 60,
    )
    arrived = lax.all_to_all(bundle, "dom", split_axis=0, concat_axis=0, tiled=True)
    total = call(
        own_kernel, "own_tiles", [HBM] * 8,
        struct((dst_blocks + 1, tile_rows, hidden), F32),
        [
            pltpu.SMEM((limit,), jnp.int32),
            pltpu.SMEM((limit,), jnp.int32),
            pltpu.SMEM((1,), jnp.int32),
            pltpu.VMEM((nodes, inputs), BF16),
            pltpu.VMEM((inputs, hidden), BF16),
            pltpu.VMEM((inputs, hidden), BF16),
            pltpu.VMEM((1, hidden), F32),
            pltpu.VMEM(adjacency.shape, BF16),
            pltpu.VMEM((dst_blocks + 1, tile_rows, hidden), BF16),
            lists,
            lists,
            pltpu.SemaphoreType.DMA((7,)),
            pltpu.SemaphoreType.DMA((limit,)),
        ],
        (tile_dst, tile_src, tile_count, features, w_self, w_neigh, bias.reshape(1, hidden), adjacency), 54,
        flops=2 * limit * tile_rows * tile_rows * hidden, size=adjacency.size * 2,
    )
    output, partial, pack = call(
        functools.partial(rest_kernel, partitions=partitions, slots=slots), "rest",
        [SMEM] * 4 + [VMEM, HBM] + [VMEM] * 4 + [HBM],
        (
            struct((nodes, hidden), BF16),
            struct((nodes, inputs), F32),
            struct((partitions, PEER_ROWS + 2 * share, inputs), F32),
        ),
        [
            pltpu.VMEM((dst_blocks + 1, tile_rows, hidden), F32),
            pltpu.VMEM((extra_blocks * tile_rows, inputs), F32),
            pltpu.VMEM((extra_blocks * tile_rows, inputs), BF16),
            pltpu.VMEM((extra_blocks + 1, tile_rows, hidden), BF16),
            pltpu.VMEM((dst_blocks, tile_rows, hidden), BF16),
            pltpu.VMEM((dst_blocks + 1, hidden, tile_rows), BF16),
            pltpu.VMEM((dst_blocks + extra_blocks + 1, hidden, tile_rows), F32),
            pltpu.VMEM((extra_blocks * tile_rows, inputs), F32),
            pltpu.VMEM(adjacency.shape, BF16),
            lists,
            lists,
            pltpu.SMEM((partitions,), jnp.int32),
            pltpu.SemaphoreType.DMA((limit,)),
            pltpu.SemaphoreType.DMA,
        ],
        (tile_dst, tile_src, tile_count, owner, arrived, total, features, w_self, w_neigh, cotangent, adjacency), 50,
    )
    returned = lax.all_to_all(pack, "dom", split_axis=0, concat_axis=0, tiled=True)
    shares, grad_bias, low = call(
        merge_kernel, "merge", [SMEM] * 4 + [VMEM] * 2,
        (
            struct((partitions, 2 * share, inputs), F32),
            struct((1, inputs), F32),
            struct((nodes, inputs), BF16),
        ),
        [pltpu.VMEM((nodes, inputs), F32), pltpu.VMEM((PEER_ROWS, inputs), F32)],
        (rows, counts, owner, hub_row, returned, partial), 32,
    )
    gathered = lax.all_to_all(shares, "dom", split_axis=0, concat_axis=0, tiled=True)
    other = lax.ppermute(low, "feat", [(0, 1), (1, 0)])
    grad_features = (low.astype(F32) + other.astype(F32)).astype(BF16)
    grad_w_self = gathered[:, :share].reshape(inputs, hidden)
    grad_w_neigh = gathered[:, share:].reshape(inputs, hidden)
    return (output, grad_features, grad_w_self, grad_w_neigh, grad_bias.reshape(hidden))


def solution(mesh):
    return jax.shard_map(
        local,
        mesh=mesh,
        in_specs=(
            P(("group", "dom"), None),
            P(None, "feat"),
            P(None, "feat"),
            P("feat"),
            P(("group", "dom"), "feat"),
            P(("group", "dom"), None, None),
            P(("group", "dom")),
            P(("group", "dom")),
            P(("group", "dom")),
            P(("group", "dom"), None, None),
            P(("group", "dom"), None),
            P("group", None),
            P("group"),
        ),
        out_specs=(
            P(("group", "dom"), "feat"),
            P(("group", "dom"), None),
            P("group", "feat"),
            P("group", "feat"),
            P(("group", "feat")),
        ),
        check_vma=False,
    )
```

```python
import functools

import jax
import jax.numpy as jnp
from jax import lax
from jax.experimental import pallas as pl
from jax.experimental.pallas import tpu as pltpu
from jax.sharding import PartitionSpec as P

HUB_MOST = 4
PEER_ROWS = 8
GROUP_TILES = 8
F32 = jnp.float32
BF16 = jnp.bfloat16
NT = (((1,), (1,)), ((), ()))


def dot(a, b):
    return jnp.dot(a, b, preferred_element_type=F32)


def dot_nt(a, b):
    return lax.dot_general(a, b, NT, preferred_element_type=F32)


def repeat(count, body, init):
    return lax.fori_loop(0, count, body, init, unroll=True)


def hub_slots(owner_ref, counter_ref, partitions, body):
    def clear(q, carry):
        counter_ref[q] = 0
        return carry

    def visit(hub, carry):
        owner = owner_ref[hub]
        slot = counter_ref[owner]
        counter_ref[owner] = slot + 1
        body(hub, owner, slot)
        return carry

    repeat(partitions, clear, 0)
    repeat(owner_ref.shape[0], visit, 0)


def fetch(pairs, sems):
    copies = [pltpu.make_async_copy(src, dst, sems.at[k]) for k, (src, dst) in enumerate(pairs)]
    for copy in copies:
        copy.start()
    return copies


def gather_kernel(
    rows_hbm, count_hbm, owner_hbm, hub_row_hbm, features_hbm,
    bundle_ref,
    rows_ref, count_ref, owner_ref, hub_row_ref, features_ref, wide_ref, hubs_ref, sems,
):
    own = lax.axis_index("dom")
    partitions = bundle_ref.shape[0]
    slots = rows_ref.shape[0]
    copies = fetch(
        [
            (features_hbm, features_ref), (rows_hbm, rows_ref), (count_hbm, count_ref),
            (owner_hbm, owner_ref), (hub_row_hbm, hub_row_ref),
        ],
        sems,
    )
    hubs_ref[...] = jnp.zeros_like(hubs_ref)
    for copy in copies:
        copy.wait()
    wide_ref[...] = features_ref[...].astype(F32)

    def hub(index, slot):
        mine = owner_ref[index] == own

        @pl.when(mine)
        def _():
            hubs_ref[pl.ds(slots + slot, 1), :] = wide_ref[pl.ds(hub_row_ref[index], 1), :]

        return slot + mine.astype(jnp.int32)

    repeat(owner_ref.shape[0], hub, jnp.int32(0))

    def peer(q, carry):
        bundle_ref[q] = hubs_ref[...]
        for slot in range(slots):
            row = wide_ref[pl.ds(rows_ref[slot, q], 1), :]
            bundle_ref[q, slot : slot + 1, :] = jnp.where(slot < count_ref[q], row, 0.0)
        return carry

    repeat(partitions, peer, 0)


def put(list_ref, position, tile, dst, src):
    list_ref[0, position] = tile
    list_ref[1, position] = dst
    list_ref[2, position] = src


def split_tiles(near_ref, far_ref, dst_ref, src_ref, count, split):
    def visit(tile, used):
        src, dst = src_ref[tile], dst_ref[tile]
        near, far = used
        put(near_ref, near, tile, dst, src)
        put(far_ref, far, tile, dst, src)
        is_near = (src < split).astype(jnp.int32)
        return near + is_near, far + 1 - is_near

    return lax.fori_loop(0, count, visit, (jnp.int32(0), jnp.int32(0)))


def pad_list(list_ref, used, dst, src):
    first = list_ref[0, 0]
    for k in range(GROUP_TILES):
        put(list_ref, used + k, first, dst, src)


class Tiles:
    def __init__(self, list_ref, total, source, held, sems):
        self.list_ref, self.total, self.source, self.held, self.sems = list_ref, total, source, held, sems

    def copy(self, position):
        tile = self.list_ref[0, position]
        return pltpu.make_async_copy(self.source.at[tile], self.held.at[tile], self.sems.at[tile])

    def start(self):
        def one(position, carry):
            self.copy(position).start()
            return carry

        lax.fori_loop(0, self.total, one, 0)

    def each(self, body, wait):
        def group(step, carry):
            if wait:
                for k in range(GROUP_TILES):
                    position = step * GROUP_TILES + k

                    @pl.when(position < self.total)
                    def _(position=position):
                        self.copy(position).wait()

            for k in range(GROUP_TILES):
                position = step * GROUP_TILES + k
                tile = self.held[self.list_ref[0, position]]
                body(tile, self.list_ref[1, position], self.list_ref[2, position])
            return carry

        lax.fori_loop(0, (self.total + GROUP_TILES - 1) // GROUP_TILES, group, 0)


def own_kernel(
    dst_hbm, src_hbm, count_hbm, features_hbm, w_self_hbm, w_neigh_hbm, bias_hbm, adjacency_hbm,
    total_ref,
    dst_ref, src_ref, count_ref, features_ref, w_self_ref, w_neigh_ref, bias_ref,
    adjacency_ref, blocks_ref, list_ref, far_list_ref, sems, tile_sems,
):
    tile_rows = adjacency_ref.shape[1]
    dst_blocks = total_ref.shape[0] - 1
    copies = fetch(
        [
            (src_hbm, src_ref), (dst_hbm, dst_ref), (count_hbm, count_ref), (w_neigh_hbm, w_neigh_ref),
            (features_hbm, features_ref), (w_self_hbm, w_self_ref), (bias_hbm, bias_ref),
        ],
        sems,
    )
    for copy in copies[:3]:
        copy.wait()
    used, _ = split_tiles(list_ref, far_list_ref, dst_ref, src_ref, count_ref[0], dst_blocks)
    pad_list(list_ref, used, dst_blocks, dst_blocks)
    tiles = Tiles(list_ref, used, adjacency_hbm, adjacency_ref, tile_sems)
    tiles.start()
    for copy in copies[3:]:
        copy.wait()
    features = features_ref[...]
    projected = dot(features, w_neigh_ref[...]).astype(BF16)
    for block in range(dst_blocks):
        blocks_ref[block] = projected[block * tile_rows : (block + 1) * tile_rows]
    blocks_ref[dst_blocks] = jnp.zeros(blocks_ref.shape[1:], BF16)
    base = dot(features, w_self_ref[...]) + bias_ref[...]
    for block in range(dst_blocks):
        total_ref[block] = base[block * tile_rows : (block + 1) * tile_rows]
    total_ref[dst_blocks] = jnp.zeros(total_ref.shape[1:], F32)

    def forward(tile, dst, src):
        total_ref[dst] += dot(tile, blocks_ref[src])

    tiles.each(forward, wait=True)


def rest_kernel(
    dst_ref, src_ref, count_ref, owner_ref,
    arrived_ref, total_hbm, features_ref, w_self_ref, w_neigh_ref, cotangent_ref, adjacency_hbm,
    output_ref, partial_ref, message_ref, keep_ref,
    halo_ref, hubs_ref, total_ref, rows_ref, low_rows_ref, blocks_ref, grad_ref, grad_t_ref, source_t_ref, back_ref,
    adjacency_ref, far_list_ref, own_list_ref, counter_ref, tile_sems, total_sem,
    *, partitions, slots,
):
    me = lax.axis_index("dom")
    tile_rows = adjacency_ref.shape[1]
    dst_blocks = total_hbm.shape[0] - 1
    halo_blocks = -(-partitions * slots // tile_rows)
    hub_blocks = -(-owner_ref.shape[0] // tile_rows)
    extra_blocks = halo_blocks + hub_blocks
    hub_base = halo_blocks * tile_rows
    source_blocks = dst_blocks + extra_blocks
    fetch_total = pltpu.make_async_copy(total_hbm, total_ref, total_sem)
    fetch_total.start()
    near_used, far_used = split_tiles(own_list_ref, far_list_ref, dst_ref, src_ref, count_ref[0], dst_blocks)
    far = Tiles(far_list_ref, far_used, adjacency_hbm, adjacency_ref, tile_sems)
    far.start()
    own = Tiles(own_list_ref, near_used, adjacency_hbm, adjacency_ref, tile_sems)
    own.start()
    pad_list(far_list_ref, far_used, dst_blocks, source_blocks)
    pad_list(own_list_ref, near_used, dst_blocks, source_blocks)

    rows_ref[...] = jnp.zeros_like(rows_ref)

    def halo_in(q, carry):
        rows_ref[pl.ds(q * slots, slots), :] = arrived_ref[q, 0:slots, :]
        return carry

    repeat(partitions, halo_in, 0)

    def hub_in(hub, owner, slot):
        rows_ref[pl.ds(hub_base + hub, 1), :] = arrived_ref[owner, pl.ds(slots + slot, 1), :]

    hub_slots(owner_ref, counter_ref, partitions, hub_in)
    low_rows_ref[...] = rows_ref[...].astype(BF16)
    for block in range(extra_blocks):
        rows = low_rows_ref[block * tile_rows : (block + 1) * tile_rows]
        blocks_ref[block] = dot(rows, w_neigh_ref[...]).astype(BF16)
    blocks_ref[extra_blocks] = jnp.zeros(blocks_ref.shape[1:], BF16)
    fetch_total.wait()

    def forward(tile, dst, src):
        total_ref[dst] += dot(tile, blocks_ref[src - dst_blocks])

    far.each(forward, wait=True)

    root = 0.7978845608028654
    bias_sum = jnp.zeros((1, output_ref.shape[1]), F32)
    w_self_t = jnp.zeros((output_ref.shape[1], features_ref.shape[1]), F32)
    for block in range(dst_blocks):
        span = slice(block * tile_rows, (block + 1) * tile_rows)
        v = total_ref[block]
        square = v * v
        gate = jnp.tanh(root * (v + 0.044715 * (v * square)))
        half = 0.5 * (1.0 + gate)
        output_ref[span, :] = (v * half).astype(BF16)
        slope = half + (0.5 * root) * v * (1.0 - gate * gate) * (1.0 + (3 * 0.044715) * square)
        grad = cotangent_ref[span, :].astype(F32) * slope
        bias_sum += jnp.sum(grad, axis=0, keepdims=True)
        low = grad.astype(BF16)
        grad_ref[block] = low
        low_t = jnp.transpose(grad).astype(BF16)
        grad_t_ref[block] = low_t
        w_self_t += dot(low_t, features_ref[span, :])
    grad_t_ref[dst_blocks] = jnp.zeros(grad_t_ref.shape[1:], BF16)

    source_t_ref[...] = jnp.zeros_like(source_t_ref)

    def backward(tile, dst, src):
        source_t_ref[src] += dot(grad_t_ref[dst], tile)

    far.each(backward, wait=False)
    own.each(backward, wait=True)

    w_neigh_t = jnp.zeros_like(w_self_t)
    for block in range(dst_blocks):
        span = slice(block * tile_rows, (block + 1) * tile_rows)
        source_t = source_t_ref[block]
        w_neigh_t += dot(source_t.astype(BF16), features_ref[span, :])
        partial_ref[span, :] = dot_nt(grad_ref[block], w_self_ref[...]) + dot_nt(
            jnp.transpose(source_t).astype(BF16), w_neigh_ref[...]
        )
    for block in range(extra_blocks):
        span = slice(block * tile_rows, (block + 1) * tile_rows)
        source_t = source_t_ref[dst_blocks + block]
        w_neigh_t += dot(source_t.astype(BF16), low_rows_ref[span, :])
        back_ref[span, :] = dot_nt(jnp.transpose(source_t).astype(BF16), w_neigh_ref[...])

    def halo_out(q, carry):
        halo_ref[pl.ds((q ^ me) * slots, slots), :] = back_ref[pl.ds(q * slots, slots), :]
        return carry

    repeat(partitions, halo_out, 0)
    hubs_ref[...] = jnp.zeros_like(hubs_ref)

    def hub_out(hub, owner, slot):
        hubs_ref[pl.ds((owner ^ me) * HUB_MOST + slot, 1), :] = back_ref[pl.ds(hub_base + hub, 1), :]

    hub_slots(owner_ref, counter_ref, partitions, hub_out)
    plan = Exchange(partitions, slots, 0)
    message_ref[0 : plan.weights, :] = jnp.concatenate([w_self_t, w_neigh_t], axis=0).astype(BF16)
    plan.write(message_ref, keep_ref, halo_ref[...], hubs_ref[...], bias_sum)


class Exchange:
    weights = 256

    def __init__(self, partitions, slots, step):
        self.groups = 1 << step
        self.half = partitions >> (step + 1)
        self.slots = slots
        self.halo = self.groups * self.half * slots
        self.hub = self.half * HUB_MOST
        self.keep = self.halo + self.hub
        self.rows = self.weights + -(-(self.keep + 2) // 16) * 16

    def halves(self, rows, width):
        lower, upper = [], []
        span = self.half * width
        for group in range(rows.shape[0] // (2 * span)):
            base = 2 * group * span
            lower.append(rows[base : base + span])
            upper.append(rows[base + span : base + 2 * span])
        return lower, upper

    def write(self, message_ref, keep_ref, halo, hubs, bias):
        halo_keep, halo_send = self.halves(halo, self.slots)
        hub_keep, hub_send = self.halves(hubs, HUB_MOST)
        high = bias.astype(BF16).astype(F32)
        spare = self.rows - self.weights - self.keep - 2
        parts = halo_send + hub_send + [high, bias - high]
        if spare:
            parts.append(jnp.zeros((spare, bias.shape[1]), F32))
        message_ref[self.weights : self.rows, :] = jnp.concatenate(parts, axis=0).astype(BF16)
        keep_ref[...] = jnp.concatenate(halo_keep + hub_keep, axis=0)

    def tail(self, ref):
        return ref[self.weights : self.rows, :].astype(F32)

    def bias(self, own, other):
        k = self.keep
        return (own[k : k + 1] + own[k + 1 : k + 2]) + (other[k : k + 1] + other[k + 1 : k + 2])

    def merged(self, keep, other):
        halo = jnp.concatenate([keep[: self.halo], other[: self.halo]], axis=0)
        return halo, keep[self.halo :] + other[self.halo : self.keep]

    def weight_sum(self, sent_ref, got_ref):
        rows = slice(0, self.weights)
        return sent_ref[rows, :].astype(F32) + got_ref[rows, :].astype(F32)


def step_kernel(sent_ref, got_ref, keep_ref, message_ref, next_keep_ref, *, now, then):
    message_ref[0 : now.weights, :] = now.weight_sum(sent_ref, got_ref).astype(BF16)
    other = now.tail(got_ref)
    halo, hubs = now.merged(keep_ref[...], other)
    then.write(message_ref, next_keep_ref, halo, hubs, now.bias(now.tail(sent_ref), other))


def returned_kernel(got_ref, keep_ref, rows_ref, *, now):
    halo, hubs = now.merged(keep_ref[...], now.tail(got_ref))
    rows_ref[...] = jnp.concatenate([halo, hubs], axis=0)


def weights_kernel(sent_ref, got_ref, w_self_ref, w_neigh_ref, bias_ref, *, now):
    total = now.weight_sum(sent_ref, got_ref)
    split = now.weights // 2
    w_self_ref[...] = jnp.transpose(total[:split])
    w_neigh_ref[...] = jnp.transpose(total[split:])
    bias_ref[...] = now.bias(now.tail(sent_ref), now.tail(got_ref))


def features_kernel(
    rows_ref, count_ref, owner_ref, hub_row_ref, partial_ref, other_partial_ref, own_rows_ref, other_rows_ref,
    low_ref, total_ref, returned_ref,
):
    me = lax.axis_index("dom")
    slots, partitions = rows_ref.shape
    steps = partitions.bit_length() - 1
    total_ref[...] = partial_ref[...] + other_partial_ref[...]
    returned_ref[...] = own_rows_ref[...] + other_rows_ref[...]

    for group in range(partitions):
        origin = me ^ sum(((group >> k) & 1) << (steps - 1 - k) for k in range(steps))
        for slot in range(slots):
            row = pl.ds(rows_ref[slot, origin], 1)
            place = group * slots + slot
            total_ref[row, :] += jnp.where(slot < count_ref[origin], returned_ref[place : place + 1, :], 0.0)

    def hub(index, slot):
        mine = owner_ref[index] == me

        @pl.when(mine)
        def _():
            total_ref[pl.ds(hub_row_ref[index], 1), :] += returned_ref[pl.ds(partitions * slots + slot, 1), :]

        return slot + mine.astype(jnp.int32)

    repeat(owner_ref.shape[0], hub, jnp.int32(0))
    low_ref[...] = total_ref[...].astype(BF16)


SMEM = pl.BlockSpec(memory_space=pltpu.SMEM)
VMEM = pl.BlockSpec(memory_space=pltpu.VMEM)
HBM = pl.BlockSpec(memory_space=pltpu.HBM)


def call(kernel, name, ins, outs, scratch, args, grant, flops=0, size=0):
    return pl.pallas_call(
        kernel,
        out_shape=outs,
        in_specs=ins,
        out_specs=jax.tree.map(lambda _: VMEM, outs),
        scratch_shapes=scratch,
        compiler_params=pltpu.CompilerParams(vmem_limit_bytes=grant * 1024 * 1024),
        cost_estimate=pl.CostEstimate(flops=flops, bytes_accessed=size, transcendentals=0),
        name=name,
    )(*args)


def local(
    features, w_self, w_neigh, bias, cotangent, adjacency, tile_dst, tile_src, tile_count,
    send_rows, send_count, hub_owner, hub_row,
):
    nodes, inputs = features.shape
    limit, tile_rows, _ = adjacency.shape
    hidden = w_neigh.shape[1]
    partitions = lax.axis_size("dom")
    slots = send_rows.shape[2]
    hubs = hub_row.shape[0]
    dst_blocks = nodes // tile_rows
    extra_blocks = -(-partitions * slots // tile_rows) - (-hubs // tile_rows)
    rows = jnp.transpose(send_rows[0])
    counts = send_count.reshape(partitions)
    owner = hub_owner.reshape(hubs)
    struct = jax.ShapeDtypeStruct
    lists = pltpu.SMEM((3, limit + GROUP_TILES), jnp.int32)

    bundle = call(
        gather_kernel, "gather", [HBM] * 5,
        struct((partitions, PEER_ROWS, inputs), F32),
        [
            pltpu.SMEM((slots, partitions), jnp.int32),
            pltpu.SMEM((partitions,), jnp.int32),
            pltpu.SMEM((hubs,), jnp.int32),
            pltpu.SMEM((hubs,), jnp.int32),
            pltpu.VMEM((nodes, inputs), BF16),
            pltpu.VMEM((nodes, inputs), F32),
            pltpu.VMEM((PEER_ROWS, inputs), F32),
            pltpu.SemaphoreType.DMA((5,)),
        ],
        (rows, counts, owner, hub_row, features), 60,
    )
    arrived = lax.all_to_all(bundle, "dom", split_axis=0, concat_axis=0, tiled=True)
    total = call(
        own_kernel, "own_tiles", [HBM] * 8,
        struct((dst_blocks + 1, tile_rows, hidden), F32),
        [
            pltpu.SMEM((limit,), jnp.int32),
            pltpu.SMEM((limit,), jnp.int32),
            pltpu.SMEM((1,), jnp.int32),
            pltpu.VMEM((nodes, inputs), BF16),
            pltpu.VMEM((inputs, hidden), BF16),
            pltpu.VMEM((inputs, hidden), BF16),
            pltpu.VMEM((1, hidden), F32),
            pltpu.VMEM(adjacency.shape, BF16),
            pltpu.VMEM((dst_blocks + 1, tile_rows, hidden), BF16),
            lists,
            lists,
            pltpu.SemaphoreType.DMA((7,)),
            pltpu.SemaphoreType.DMA((limit,)),
        ],
        (tile_dst, tile_src, tile_count, features, w_self, w_neigh, bias.reshape(1, hidden), adjacency), 54,
        flops=2 * limit * tile_rows * tile_rows * hidden, size=adjacency.size * 2,
    )
    plans = [Exchange(partitions, slots, step) for step in range(partitions.bit_length() - 1)]
    output, partial, message, keep = call(
        functools.partial(rest_kernel, partitions=partitions, slots=slots), "rest",
        [SMEM] * 4 + [VMEM, HBM] + [VMEM] * 4 + [HBM],
        (
            struct((nodes, hidden), BF16),
            struct((nodes, inputs), F32),
            struct((plans[0].rows, inputs), BF16),
            struct((plans[0].keep, inputs), F32),
        ),
        [
            pltpu.VMEM((partitions * slots, inputs), F32),
            pltpu.VMEM((partitions * HUB_MOST, inputs), F32),
            pltpu.VMEM((dst_blocks + 1, tile_rows, hidden), F32),
            pltpu.VMEM((extra_blocks * tile_rows, inputs), F32),
            pltpu.VMEM((extra_blocks * tile_rows, inputs), BF16),
            pltpu.VMEM((extra_blocks + 1, tile_rows, hidden), BF16),
            pltpu.VMEM((dst_blocks, tile_rows, hidden), BF16),
            pltpu.VMEM((dst_blocks + 1, hidden, tile_rows), BF16),
            pltpu.VMEM((dst_blocks + extra_blocks + 1, hidden, tile_rows), F32),
            pltpu.VMEM((extra_blocks * tile_rows, inputs), F32),
            pltpu.VMEM(adjacency.shape, BF16),
            lists,
            lists,
            pltpu.SMEM((partitions,), jnp.int32),
            pltpu.SemaphoreType.DMA((limit,)),
            pltpu.SemaphoreType.DMA,
        ],
        (tile_dst, tile_src, tile_count, owner, arrived, total, features, w_self, w_neigh, cotangent, adjacency), 50,
    )
    other_partial = lax.ppermute(partial, "feat", [(0, 1), (1, 0)])
    for now in plans:
        got = lax.ppermute(message, "dom", [(q, q ^ now.half) for q in range(partitions)])
        if now is plans[-1]:
            break
        then = plans[plans.index(now) + 1]
        message, keep = call(
            functools.partial(step_kernel, now=now, then=then), "step", [VMEM] * 3,
            (struct((then.rows, inputs), BF16), struct((then.keep, inputs), F32)),
            [], (message, got, keep), 16,
        )
    own_rows = call(
        functools.partial(returned_kernel, now=now), "returned", [VMEM] * 2,
        struct((2 * now.halo + now.hub, inputs), F32), [], (got, keep), 16,
    )
    other_rows = lax.ppermute(own_rows, "feat", [(0, 1), (1, 0)])
    grad_w_self, grad_w_neigh, grad_bias = call(
        functools.partial(weights_kernel, now=now), "weights", [VMEM] * 2,
        (struct((inputs, hidden), F32), struct((inputs, hidden), F32), struct((1, hidden), F32)),
        [], (message, got), 16,
    )
    grad_features = call(
        features_kernel, "features", [SMEM] * 4 + [VMEM] * 4, struct((nodes, inputs), BF16),
        [pltpu.VMEM((nodes, inputs), F32), pltpu.VMEM((2 * now.halo + now.hub, inputs), F32)],
        (rows, counts, owner, hub_row, partial, other_partial, own_rows, other_rows), 32,
    )
    return (output, grad_features, grad_w_self, grad_w_neigh, grad_bias.reshape(hidden))


def solution(mesh):
    return jax.shard_map(
        local,
        mesh=mesh,
        in_specs=(
            P(("group", "dom"), None),
            P(None, "feat"),
            P(None, "feat"),
            P("feat"),
            P(("group", "dom"), "feat"),
            P(("group", "dom"), None, None),
            P(("group", "dom")),
            P(("group", "dom")),
            P(("group", "dom")),
            P(("group", "dom"), None, None),
            P(("group", "dom"), None),
            P("group", None),
            P("group"),
        ),
        out_specs=(
            P(("group", "dom"), "feat"),
            P(("group", "dom"), None),
            P("group", "feat"),
            P("group", "feat"),
            P(("group", "feat")),
        ),
        check_vma=False,
    )
```

```python
import functools

import jax
import jax.numpy as jnp
from jax import lax
from jax.experimental import pallas as pl
from jax.experimental.pallas import tpu as pltpu
from jax.sharding import PartitionSpec as P

HUB_MOST = 4
PEER_ROWS = 8
GROUP_TILES = 8
F32 = jnp.float32
BF16 = jnp.bfloat16
NT = (((1,), (1,)), ((), ()))


def dot(a, b):
    return jnp.dot(a, b, preferred_element_type=F32)


def dot_nt(a, b):
    return lax.dot_general(a, b, NT, preferred_element_type=F32)


def repeat(count, body, init):
    return lax.fori_loop(0, count, body, init, unroll=True)


def hub_slots(owner_ref, counter_ref, partitions, body):
    def clear(q, carry):
        counter_ref[q] = 0
        return carry

    def visit(hub, carry):
        owner = owner_ref[hub]
        slot = counter_ref[owner]
        counter_ref[owner] = slot + 1
        body(hub, owner, slot)
        return carry

    repeat(partitions, clear, 0)
    repeat(owner_ref.shape[0], visit, 0)


def fetch(pairs, sems):
    copies = [pltpu.make_async_copy(src, dst, sems.at[k]) for k, (src, dst) in enumerate(pairs)]
    for copy in copies:
        copy.start()
    return copies


def gather_kernel(
    rows_hbm, count_hbm, owner_hbm, hub_row_hbm, features_hbm,
    bundle_ref,
    rows_ref, count_ref, owner_ref, hub_row_ref, features_ref, wide_ref, hubs_ref, sems,
):
    own = lax.axis_index("dom")
    partitions = bundle_ref.shape[0]
    slots = rows_ref.shape[0]
    copies = fetch(
        [
            (features_hbm, features_ref), (rows_hbm, rows_ref), (count_hbm, count_ref),
            (owner_hbm, owner_ref), (hub_row_hbm, hub_row_ref),
        ],
        sems,
    )
    hubs_ref[...] = jnp.zeros_like(hubs_ref)
    for copy in copies:
        copy.wait()
    wide_ref[...] = features_ref[...].astype(F32)

    def hub(index, slot):
        mine = owner_ref[index] == own

        @pl.when(mine)
        def _():
            hubs_ref[pl.ds(slots + slot, 1), :] = wide_ref[pl.ds(hub_row_ref[index], 1), :]

        return slot + mine.astype(jnp.int32)

    repeat(owner_ref.shape[0], hub, jnp.int32(0))

    def peer(q, carry):
        bundle_ref[q] = hubs_ref[...]
        for slot in range(slots):
            row = wide_ref[pl.ds(rows_ref[slot, q], 1), :]
            bundle_ref[q, slot : slot + 1, :] = jnp.where(slot < count_ref[q], row, 0.0)
        return carry

    repeat(partitions, peer, 0)


def put(list_ref, position, tile, dst, src):
    list_ref[0, position] = tile
    list_ref[1, position] = dst
    list_ref[2, position] = src


def split_tiles(near_ref, far_ref, dst_ref, src_ref, count, split):
    def visit(tile, used):
        src, dst = src_ref[tile], dst_ref[tile]
        near, far = used
        put(near_ref, near, tile, dst, src)
        put(far_ref, far, tile, dst, src)
        is_near = (src < split).astype(jnp.int32)
        return near + is_near, far + 1 - is_near

    return lax.fori_loop(0, count, visit, (jnp.int32(0), jnp.int32(0)))


def pad_list(list_ref, used, dst, src):
    first = list_ref[0, 0]
    for k in range(GROUP_TILES):
        put(list_ref, used + k, first, dst, src)


class Tiles:
    def __init__(self, list_ref, total, source, held, sems, columns=None):
        self.list_ref, self.total, self.source, self.held, self.sems = list_ref, total, source, held, sems
        self.columns = held.shape[2] if columns is None else columns

    def copy(self, position):
        tile = self.list_ref[0, position]
        span = slice(0, self.columns)
        return pltpu.make_async_copy(
            self.source.at[tile, :, span], self.held.at[tile, :, span], self.sems.at[tile]
        )

    def start(self):
        def one(position, carry):
            self.copy(position).start()
            return carry

        lax.fori_loop(0, self.total, one, 0)

    def each(self, body):
        def group(step, carry):
            for k in range(GROUP_TILES):
                position = step * GROUP_TILES + k

                @pl.when(position < self.total)
                def _(position=position):
                    self.copy(position).wait()

            for k in range(GROUP_TILES):
                position = step * GROUP_TILES + k
                tile = self.held[self.list_ref[0, position]]
                body(tile, self.list_ref[1, position], self.list_ref[2, position])
            return carry

        lax.fori_loop(0, (self.total + GROUP_TILES - 1) // GROUP_TILES, group, 0)


def own_kernel(
    dst_hbm, src_hbm, count_hbm, features_hbm, w_self_hbm, w_neigh_hbm, bias_hbm, adjacency_hbm,
    total_hbm, far_hbm,
    dst_ref, src_ref, count_ref, features_ref, w_self_ref, w_neigh_ref, bias_ref,
    adjacency_ref, blocks_ref, total_ref, sums_ref, far_ref, list_ref, far_list_ref, sems, tile_sems, out_sems,
):
    tile_rows = adjacency_ref.shape[1]
    dst_blocks = total_ref.shape[0] - 1
    far_blocks, columns = sums_ref.shape[1], sums_ref.shape[3]
    copies = fetch(
        [
            (src_hbm, src_ref), (dst_hbm, dst_ref), (count_hbm, count_ref), (w_neigh_hbm, w_neigh_ref),
            (features_hbm, features_ref), (w_self_hbm, w_self_ref), (bias_hbm, bias_ref),
        ],
        sems,
    )
    sums_ref[...] = jnp.zeros_like(sums_ref)
    for copy in copies[:3]:
        copy.wait()
    near_used, far_used = split_tiles(list_ref, far_list_ref, dst_ref, src_ref, count_ref[0], dst_blocks)
    far = Tiles(far_list_ref, far_used, adjacency_hbm, adjacency_ref, tile_sems, columns)
    far.start()
    near = Tiles(list_ref, near_used, adjacency_hbm, adjacency_ref, tile_sems)
    near.start()
    pad_list(list_ref, near_used, dst_blocks, dst_blocks)
    for copy in copies[3:]:
        copy.wait()
    features = features_ref[...]
    projected = dot(features, w_neigh_ref[...]).astype(BF16)
    for block in range(dst_blocks):
        blocks_ref[block] = projected[block * tile_rows : (block + 1) * tile_rows]
    blocks_ref[dst_blocks] = jnp.zeros(blocks_ref.shape[1:], BF16)
    base = dot(features, w_self_ref[...]) + bias_ref[...]
    for block in range(dst_blocks):
        total_ref[block] = base[block * tile_rows : (block + 1) * tile_rows]
    total_ref[dst_blocks] = jnp.zeros(total_ref.shape[1:], F32)

    def add_far(position, carry):
        far.copy(position).wait()
        tile = adjacency_ref[far_list_ref[0, position], :, :columns]
        sums_ref[far_list_ref[1, position], far_list_ref[2, position] - dst_blocks] += tile.astype(F32)
        return carry

    lax.fori_loop(0, far_used, add_far, 0)
    for dst in range(dst_blocks):
        for block in range(far_blocks):
            far_ref[dst, :, block * columns : (block + 1) * columns] = sums_ref[dst, block].astype(BF16)
    far_out = pltpu.make_async_copy(far_ref, far_hbm.at[0:dst_blocks], out_sems.at[0])
    far_out.start()

    def forward(tile, dst, src):
        total_ref[dst] += dot(tile, blocks_ref[src])

    near.each(forward)
    total_out = pltpu.make_async_copy(total_ref.at[0:dst_blocks], total_hbm.at[0:dst_blocks], out_sems.at[1])
    total_out.start()
    far_out.wait()
    total_out.wait()


def rest_kernel(
    dst_ref, src_ref, count_ref, owner_ref,
    arrived_ref, total_hbm, far_hbm, features_ref, w_self_ref, w_neigh_ref, cotangent_ref, adjacency_hbm,
    output_hbm, partial_ref, message_ref, keep_ref,
    halo_ref, hubs_ref, output_ref, total_ref, far_ref, rows_ref, low_rows_ref, grad_ref, grad_t_ref, source_t_ref,
    back_ref, adjacency_ref, list_ref, counter_ref, tile_sems, sems,
    *, partitions, slots, columns,
):
    me = lax.axis_index("dom")
    tile_rows = adjacency_ref.shape[1]
    dst_blocks = total_ref.shape[0]
    halo_blocks = -(-partitions * slots // tile_rows)
    hub_base = halo_blocks * columns
    total_in = pltpu.make_async_copy(total_hbm.at[0:dst_blocks], total_ref, sems.at[0])
    total_in.start()
    far_in = pltpu.make_async_copy(far_hbm.at[0:dst_blocks], far_ref, sems.at[1])
    far_in.start()

    def find_near(tile, used):
        src = src_ref[tile]
        is_near = src < dst_blocks
        put(list_ref, used, tile, dst_ref[tile], src)

        @pl.when(is_near)
        def _():
            pltpu.make_async_copy(adjacency_hbm.at[tile], adjacency_ref.at[tile], tile_sems.at[tile]).start()

        return used + is_near.astype(jnp.int32)

    used = lax.fori_loop(0, count_ref[0], find_near, jnp.int32(0))
    near = Tiles(list_ref, used, adjacency_hbm, adjacency_ref, tile_sems)
    pad_list(list_ref, used, dst_blocks, dst_blocks)

    rows_ref[...] = jnp.zeros_like(rows_ref)

    def halo_in(q, carry):
        rows_ref[pl.ds(q * slots, slots), :] = arrived_ref[q, 0:slots, :]
        return carry

    repeat(partitions, halo_in, 0)

    def hub_in(hub, owner, slot):
        rows_ref[pl.ds(hub_base + hub, 1), :] = arrived_ref[owner, pl.ds(slots + slot, 1), :]

    hub_slots(owner_ref, counter_ref, partitions, hub_in)
    low_rows = rows_ref[...].astype(BF16)
    low_rows_ref[...] = low_rows
    far_projected = dot(low_rows, w_neigh_ref[...]).astype(BF16)
    total_in.wait()
    far_in.wait()

    root = 0.7978845608028654
    bias_sum = jnp.zeros((1, output_ref.shape[1]), F32)
    for block in range(dst_blocks):
        span = slice(block * tile_rows, (block + 1) * tile_rows)
        v = total_ref[block] + dot(far_ref[block], far_projected)
        square = v * v
        gate = jnp.tanh(root * (v + 0.044715 * (v * square)))
        half = 0.5 * (1.0 + gate)
        output_ref[span, :] = (v * half).astype(BF16)
        slope = half + (0.5 * root) * v * (1.0 - gate * gate) * (1.0 + (3 * 0.044715) * square)
        grad = cotangent_ref[span, :].astype(F32) * slope
        bias_sum += jnp.sum(grad, axis=0, keepdims=True)
        grad_ref[block] = grad.astype(BF16)
        grad_t_ref[block] = jnp.transpose(grad).astype(BF16)
    output_out = pltpu.make_async_copy(output_ref, output_hbm, sems.at[2])
    output_out.start()
    grad_t_ref[dst_blocks] = jnp.zeros(grad_t_ref.shape[1:], BF16)
    source_t_ref[...] = jnp.zeros_like(source_t_ref)

    def backward(tile, dst, src):
        source_t_ref[src] += dot(grad_t_ref[dst], tile)

    near.each(backward)

    far_t = jnp.zeros((output_ref.shape[1], far_ref.shape[2]), F32)
    for block in range(dst_blocks):
        far_t += dot(grad_t_ref[block], far_ref[block])
    back_ref[...] = dot_nt(jnp.transpose(far_t).astype(BF16), w_neigh_ref[...])
    w_self_t = jnp.zeros((output_ref.shape[1], features_ref.shape[1]), F32)
    w_neigh_t = dot(far_t.astype(BF16), low_rows_ref[...])
    for block in range(dst_blocks):
        span = slice(block * tile_rows, (block + 1) * tile_rows)
        source_t = source_t_ref[block]
        w_self_t += dot(grad_t_ref[block], features_ref[span, :])
        w_neigh_t += dot(source_t.astype(BF16), features_ref[span, :])
        partial_ref[span, :] = dot_nt(grad_ref[block], w_self_ref[...]) + dot_nt(
            jnp.transpose(source_t).astype(BF16), w_neigh_ref[...]
        )

    def halo_out(q, carry):
        halo_ref[pl.ds((q ^ me) * slots, slots), :] = back_ref[pl.ds(q * slots, slots), :]
        return carry

    repeat(partitions, halo_out, 0)
    hubs_ref[...] = jnp.zeros_like(hubs_ref)

    def hub_out(hub, owner, slot):
        hubs_ref[pl.ds((owner ^ me) * HUB_MOST + slot, 1), :] = back_ref[pl.ds(hub_base + hub, 1), :]

    hub_slots(owner_ref, counter_ref, partitions, hub_out)
    plan = Exchange(partitions, slots, 0)
    message_ref[0 : plan.weights, :] = jnp.concatenate([w_self_t, w_neigh_t], axis=0).astype(BF16)
    plan.write(message_ref, keep_ref, halo_ref[...], hubs_ref[...], bias_sum)
    output_out.wait()


class Exchange:
    weights = 256

    def __init__(self, partitions, slots, step):
        self.groups = 1 << step
        self.half = partitions >> (step + 1)
        self.slots = slots
        self.halo = self.groups * self.half * slots
        self.hub = self.half * HUB_MOST
        self.keep = self.halo + self.hub
        self.rows = self.weights + -(-(self.keep + 2) // 16) * 16

    def halves(self, rows, width):
        lower, upper = [], []
        span = self.half * width
        for group in range(rows.shape[0] // (2 * span)):
            base = 2 * group * span
            lower.append(rows[base : base + span])
            upper.append(rows[base + span : base + 2 * span])
        return lower, upper

    def write(self, message_ref, keep_ref, halo, hubs, bias):
        halo_keep, halo_send = self.halves(halo, self.slots)
        hub_keep, hub_send = self.halves(hubs, HUB_MOST)
        high = bias.astype(BF16).astype(F32)
        spare = self.rows - self.weights - self.keep - 2
        parts = halo_send + hub_send + [high, bias - high]
        if spare:
            parts.append(jnp.zeros((spare, bias.shape[1]), F32))
        message_ref[self.weights : self.rows, :] = jnp.concatenate(parts, axis=0).astype(BF16)
        keep_ref[...] = jnp.concatenate(halo_keep + hub_keep, axis=0)

    def tail(self, ref):
        return ref[self.weights : self.rows, :].astype(F32)

    def bias(self, own, other):
        k = self.keep
        return (own[k : k + 1] + own[k + 1 : k + 2]) + (other[k : k + 1] + other[k + 1 : k + 2])

    def merged(self, keep, other):
        halo = jnp.concatenate([keep[: self.halo], other[: self.halo]], axis=0)
        return halo, keep[self.halo :] + other[self.halo : self.keep]

    def weight_sum(self, sent_ref, got_ref):
        rows = slice(0, self.weights)
        return sent_ref[rows, :].astype(F32) + got_ref[rows, :].astype(F32)


def step_kernel(sent_ref, got_ref, keep_ref, message_ref, next_keep_ref, *, now, then):
    message_ref[0 : now.weights, :] = now.weight_sum(sent_ref, got_ref).astype(BF16)
    other = now.tail(got_ref)
    halo, hubs = now.merged(keep_ref[...], other)
    then.write(message_ref, next_keep_ref, halo, hubs, now.bias(now.tail(sent_ref), other))


def returned_kernel(got_ref, keep_ref, rows_ref, *, now):
    halo, hubs = now.merged(keep_ref[...], now.tail(got_ref))
    rows_ref[...] = jnp.concatenate([halo, hubs], axis=0)


def weights_kernel(sent_ref, got_ref, w_self_ref, w_neigh_ref, bias_ref, *, now):
    total = now.weight_sum(sent_ref, got_ref)
    split = now.weights // 2
    w_self_ref[...] = jnp.transpose(total[:split])
    w_neigh_ref[...] = jnp.transpose(total[split:])
    bias_ref[...] = now.bias(now.tail(sent_ref), now.tail(got_ref))


def features_kernel(
    rows_ref, count_ref, owner_ref, hub_row_ref, partial_ref, other_partial_ref, own_rows_ref, other_rows_ref,
    low_ref, total_ref, returned_ref,
):
    me = lax.axis_index("dom")
    slots, partitions = rows_ref.shape
    steps = partitions.bit_length() - 1
    total_ref[...] = partial_ref[...] + other_partial_ref[...]
    returned_ref[...] = own_rows_ref[...] + other_rows_ref[...]

    for group in range(partitions):
        origin = me ^ sum(((group >> k) & 1) << (steps - 1 - k) for k in range(steps))
        for slot in range(slots):
            row = pl.ds(rows_ref[slot, origin], 1)
            place = group * slots + slot
            total_ref[row, :] += jnp.where(slot < count_ref[origin], returned_ref[place : place + 1, :], 0.0)

    def hub(index, slot):
        mine = owner_ref[index] == me

        @pl.when(mine)
        def _():
            total_ref[pl.ds(hub_row_ref[index], 1), :] += returned_ref[pl.ds(partitions * slots + slot, 1), :]

        return slot + mine.astype(jnp.int32)

    repeat(owner_ref.shape[0], hub, jnp.int32(0))
    low_ref[...] = total_ref[...].astype(BF16)


SMEM = pl.BlockSpec(memory_space=pltpu.SMEM)
VMEM = pl.BlockSpec(memory_space=pltpu.VMEM)
HBM = pl.BlockSpec(memory_space=pltpu.HBM)


def call(kernel, name, ins, outs, scratch, args, grant, flops=0, size=0, out_specs=None):
    return pl.pallas_call(
        kernel,
        out_shape=outs,
        in_specs=ins,
        out_specs=jax.tree.map(lambda _: VMEM, outs) if out_specs is None else out_specs,
        scratch_shapes=scratch,
        compiler_params=pltpu.CompilerParams(vmem_limit_bytes=grant * 1024 * 1024),
        cost_estimate=pl.CostEstimate(flops=flops, bytes_accessed=size, transcendentals=0),
        name=name,
    )(*args)


def local(
    features, w_self, w_neigh, bias, cotangent, adjacency, tile_dst, tile_src, tile_count,
    send_rows, send_count, hub_owner, hub_row,
):
    nodes, inputs = features.shape
    limit, tile_rows, _ = adjacency.shape
    hidden = w_neigh.shape[1]
    partitions = lax.axis_size("dom")
    slots = send_rows.shape[2]
    hubs = hub_row.shape[0]
    dst_blocks = nodes // tile_rows
    far_blocks = -(-partitions * slots // tile_rows) - (-hubs // tile_rows)
    columns = min(tile_rows, -(-max(partitions * slots, hubs) // 128) * 128)
    rows = jnp.transpose(send_rows[0])
    counts = send_count.reshape(partitions)
    owner = hub_owner.reshape(hubs)
    struct = jax.ShapeDtypeStruct
    lists = pltpu.SMEM((3, limit + GROUP_TILES), jnp.int32)

    bundle = call(
        gather_kernel, "gather", [HBM] * 5,
        struct((partitions, PEER_ROWS, inputs), F32),
        [
            pltpu.SMEM((slots, partitions), jnp.int32),
            pltpu.SMEM((partitions,), jnp.int32),
            pltpu.SMEM((hubs,), jnp.int32),
            pltpu.SMEM((hubs,), jnp.int32),
            pltpu.VMEM((nodes, inputs), BF16),
            pltpu.VMEM((nodes, inputs), F32),
            pltpu.VMEM((PEER_ROWS, inputs), F32),
            pltpu.SemaphoreType.DMA((5,)),
        ],
        (rows, counts, owner, hub_row, features), 60,
    )
    arrived = lax.all_to_all(bundle, "dom", split_axis=0, concat_axis=0, tiled=True)
    total, far = call(
        own_kernel, "own_tiles", [HBM] * 8,
        (
            struct((limit, tile_rows, hidden), F32),
            struct((limit, tile_rows, far_blocks * columns), BF16),
        ),
        [
            pltpu.SMEM((limit,), jnp.int32),
            pltpu.SMEM((limit,), jnp.int32),
            pltpu.SMEM((1,), jnp.int32),
            pltpu.VMEM((nodes, inputs), BF16),
            pltpu.VMEM((inputs, hidden), BF16),
            pltpu.VMEM((inputs, hidden), BF16),
            pltpu.VMEM((1, hidden), F32),
            pltpu.VMEM(adjacency.shape, BF16),
            pltpu.VMEM((dst_blocks + 1, tile_rows, hidden), BF16),
            pltpu.VMEM((dst_blocks + 1, tile_rows, hidden), F32),
            pltpu.VMEM((dst_blocks, far_blocks, tile_rows, columns), F32),
            pltpu.VMEM((dst_blocks, tile_rows, far_blocks * columns), BF16),
            lists,
            lists,
            pltpu.SemaphoreType.DMA((7,)),
            pltpu.SemaphoreType.DMA((limit,)),
            pltpu.SemaphoreType.DMA((2,)),
        ],
        (tile_dst, tile_src, tile_count, features, w_self, w_neigh, bias.reshape(1, hidden), adjacency),
        54, flops=2 * limit * tile_rows * tile_rows * hidden, size=adjacency.size * 2, out_specs=(HBM, HBM),
    )
    plans = [Exchange(partitions, slots, step) for step in range(partitions.bit_length() - 1)]
    output, partial, message, keep = call(
        functools.partial(rest_kernel, partitions=partitions, slots=slots, columns=columns), "rest",
        [SMEM] * 4 + [VMEM, HBM, HBM] + [VMEM] * 4 + [HBM],
        (
            struct((nodes, hidden), BF16),
            struct((nodes, inputs), F32),
            struct((plans[0].rows, inputs), BF16),
            struct((plans[0].keep, inputs), F32),
        ),
        [
            pltpu.VMEM((partitions * slots, inputs), F32),
            pltpu.VMEM((partitions * HUB_MOST, inputs), F32),
            pltpu.VMEM((nodes, hidden), BF16),
            pltpu.VMEM((dst_blocks, tile_rows, hidden), F32),
            pltpu.VMEM((dst_blocks, tile_rows, far_blocks * columns), BF16),
            pltpu.VMEM((far_blocks * columns, inputs), F32),
            pltpu.VMEM((far_blocks * columns, inputs), BF16),
            pltpu.VMEM((dst_blocks, tile_rows, hidden), BF16),
            pltpu.VMEM((dst_blocks + 1, hidden, tile_rows), BF16),
            pltpu.VMEM((dst_blocks + 1, hidden, tile_rows), F32),
            pltpu.VMEM((far_blocks * columns, inputs), F32),
            pltpu.VMEM(adjacency.shape, BF16),
            lists,
            pltpu.SMEM((partitions,), jnp.int32),
            pltpu.SemaphoreType.DMA((limit,)),
            pltpu.SemaphoreType.DMA((3,)),
        ],
        (
            tile_dst, tile_src, tile_count, owner,
            arrived, total, far, features, w_self, w_neigh, cotangent, adjacency,
        ),
        50, out_specs=(HBM, VMEM, VMEM, VMEM),
    )
    other_partial = lax.ppermute(partial, "feat", [(0, 1), (1, 0)])
    for now in plans:
        got = lax.ppermute(message, "dom", [(q, q ^ now.half) for q in range(partitions)])
        if now is plans[-1]:
            break
        then = plans[plans.index(now) + 1]
        message, keep = call(
            functools.partial(step_kernel, now=now, then=then), "step", [VMEM] * 3,
            (struct((then.rows, inputs), BF16), struct((then.keep, inputs), F32)),
            [], (message, got, keep), 16,
        )
    own_rows = call(
        functools.partial(returned_kernel, now=now), "returned", [VMEM] * 2,
        struct((2 * now.halo + now.hub, inputs), F32), [], (got, keep), 16,
    )
    other_rows = lax.ppermute(own_rows, "feat", [(0, 1), (1, 0)])
    grad_w_self, grad_w_neigh, grad_bias = call(
        functools.partial(weights_kernel, now=now), "weights", [VMEM] * 2,
        (struct((inputs, hidden), F32), struct((inputs, hidden), F32), struct((1, hidden), F32)),
        [], (message, got), 16,
    )
    grad_features = call(
        features_kernel, "features", [SMEM] * 4 + [VMEM] * 4, struct((nodes, inputs), BF16),
        [pltpu.VMEM((nodes, inputs), F32), pltpu.VMEM((2 * now.halo + now.hub, inputs), F32)],
        (rows, counts, owner, hub_row, partial, other_partial, own_rows, other_rows), 32,
    )
    return (output, grad_features, grad_w_self, grad_w_neigh, grad_bias.reshape(hidden))


def solution(mesh):
    return jax.shard_map(
        local,
        mesh=mesh,
        in_specs=(
            P(("group", "dom"), None),
            P(None, "feat"),
            P(None, "feat"),
            P("feat"),
            P(("group", "dom"), "feat"),
            P(("group", "dom"), None, None),
            P(("group", "dom")),
            P(("group", "dom")),
            P(("group", "dom")),
            P(("group", "dom"), None, None),
            P(("group", "dom"), None),
            P("group", None),
            P("group"),
        ),
        out_specs=(
            P(("group", "dom"), "feat"),
            P(("group", "dom"), None),
            P("group", "feat"),
            P("group", "feat"),
            P(("group", "feat")),
        ),
        check_vma=False,
    )
```

```python
import functools

import jax
import jax.numpy as jnp
from jax import lax
from jax.experimental import pallas as pl
from jax.experimental.pallas import tpu as pltpu
from jax.sharding import PartitionSpec as P

HUB_MOST = 4
PEER_ROWS = 8
GROUP_TILES = 8
FAR_GROUP = 4
F32 = jnp.float32
BF16 = jnp.bfloat16
NT = (((1,), (1,)), ((), ()))


def dot(a, b):
    return jnp.dot(a, b, preferred_element_type=F32)


def dot_nt(a, b):
    return lax.dot_general(a, b, NT, preferred_element_type=F32)


def repeat(count, body, init):
    return lax.fori_loop(0, count, body, init, unroll=True)


def hub_slots(owner_ref, counter_ref, partitions, body):
    def clear(q, carry):
        counter_ref[q] = 0
        return carry

    def visit(hub, carry):
        owner = owner_ref[hub]
        slot = counter_ref[owner]
        counter_ref[owner] = slot + 1
        body(hub, owner, slot)
        return carry

    repeat(partitions, clear, 0)
    repeat(owner_ref.shape[0], visit, 0)


def fetch(pairs, sems):
    copies = [pltpu.make_async_copy(src, dst, sems.at[k]) for k, (src, dst) in enumerate(pairs)]
    for copy in copies:
        copy.start()
    return copies


def gather_kernel(
    rows_hbm, count_hbm, owner_hbm, hub_row_hbm, features_hbm,
    bundle_ref,
    rows_ref, count_ref, owner_ref, hub_row_ref, features_ref, wide_ref, hubs_ref, sems,
):
    own = lax.axis_index("dom")
    partitions = bundle_ref.shape[0]
    slots = rows_ref.shape[0]
    copies = fetch(
        [
            (features_hbm, features_ref), (rows_hbm, rows_ref), (count_hbm, count_ref),
            (owner_hbm, owner_ref), (hub_row_hbm, hub_row_ref),
        ],
        sems,
    )
    hubs_ref[...] = jnp.zeros_like(hubs_ref)
    for copy in copies:
        copy.wait()
    wide_ref[...] = features_ref[...].astype(F32)

    def hub(index, slot):
        hubs_ref[pl.ds(slots + slot, 1), :] = wide_ref[pl.ds(hub_row_ref[index], 1), :]
        return slot + (owner_ref[index] == own).astype(jnp.int32)

    repeat(owner_ref.shape[0], hub, jnp.int32(0))

    def peer(q, carry):
        bundle_ref[q] = hubs_ref[...]
        for slot in range(slots):
            row = wide_ref[pl.ds(rows_ref[slot, q], 1), :]
            bundle_ref[q, slot : slot + 1, :] = jnp.where(slot < count_ref[q], row, 0.0)
        return carry

    repeat(partitions, peer, 0)


def pack_tile(tile, dst, src):
    return tile + (dst << 8) + (src << 16)


def pad_list(list_ref, used, dst, src, group):
    spare = pack_tile(list_ref[0] & 255, dst, src)
    for k in range(group):
        list_ref[used + k] = spare


class Tiles:
    def __init__(self, list_ref, source, held, sems, columns=None):
        self.list_ref, self.source, self.held, self.sems = list_ref, source, held, sems
        self.columns = held.shape[2] if columns is None else columns

    def copy(self, tile):
        span = slice(0, self.columns)
        return pltpu.make_async_copy(
            self.source.at[tile, :, span], self.held.at[tile, :, span], self.sems.at[tile]
        )

    def start(self, total):
        def one(position, carry):
            self.copy(self.list_ref[position] & 255).start()
            return carry

        lax.fori_loop(0, total, one, 0)

    def each(self, total, size, body):
        def group(step, carry):
            codes = [self.list_ref[step * size + k] for k in range(size)]
            for k in range(size):

                @pl.when(step * size + k < total)
                def _(k=k):
                    self.copy(codes[k] & 255).wait()

            for code in codes:
                body(code & 255, (code >> 8) & 255, code >> 16)
            return carry

        lax.fori_loop(0, (total + size - 1) // size, group, 0)


def own_kernel(
    dst_hbm, src_hbm, count_hbm, features_hbm, w_self_hbm, w_neigh_hbm, bias_hbm, adjacency_hbm,
    total_hbm, far_hbm,
    dst_ref, src_ref, count_ref, features_ref, w_self_ref, w_neigh_ref, bias_ref,
    adjacency_ref, blocks_ref, total_ref, sums_ref, far_ref, list_ref, far_list_ref, sems, tile_sems, out_sems,
):
    tile_rows = adjacency_ref.shape[1]
    dst_blocks = total_ref.shape[0] - 1
    far_blocks, columns = sums_ref.shape[1], sums_ref.shape[3]
    copies = fetch(
        [
            (src_hbm, src_ref), (dst_hbm, dst_ref), (count_hbm, count_ref), (w_neigh_hbm, w_neigh_ref),
            (features_hbm, features_ref), (w_self_hbm, w_self_ref), (bias_hbm, bias_ref),
        ],
        sems,
    )
    sums_ref[...] = jnp.zeros_like(sums_ref)
    for copy in copies[:3]:
        copy.wait()
    far = Tiles(far_list_ref, adjacency_hbm, adjacency_ref, tile_sems, columns)
    near = Tiles(list_ref, adjacency_hbm, adjacency_ref, tile_sems)

    def split(tile, used):
        near_used, far_used = used
        code = pack_tile(tile, dst_ref[tile], src_ref[tile])
        list_ref[near_used] = code
        far_list_ref[far_used] = code
        is_near = (code < (dst_blocks << 16)).astype(jnp.int32)

        @pl.when(is_near == 0)
        def _():
            far.copy(tile).start()

        return near_used + is_near, far_used + 1 - is_near

    near_used, far_used = lax.fori_loop(0, count_ref[0], split, (jnp.int32(0), jnp.int32(0)))
    near.start(near_used)
    pad_list(list_ref, near_used, dst_blocks, dst_blocks, GROUP_TILES)
    pad_list(far_list_ref, far_used, dst_blocks, dst_blocks, FAR_GROUP)
    for copy in copies[3:]:
        copy.wait()
    features = features_ref[...]
    projected = dot(features, w_neigh_ref[...]).astype(BF16)
    for block in range(dst_blocks):
        blocks_ref[block] = projected[block * tile_rows : (block + 1) * tile_rows]
    blocks_ref[dst_blocks] = jnp.zeros(blocks_ref.shape[1:], BF16)
    base = dot(features, w_self_ref[...]) + bias_ref[...]
    for block in range(dst_blocks):
        total_ref[block] = base[block * tile_rows : (block + 1) * tile_rows]
    total_ref[dst_blocks] = jnp.zeros(total_ref.shape[1:], F32)

    def add_far(tile, dst, src):
        sums_ref[dst, src - dst_blocks] += adjacency_ref[tile, :, :columns].astype(F32)

    far.each(far_used, FAR_GROUP, add_far)
    for dst in range(dst_blocks):
        for block in range(far_blocks):
            far_ref[dst, :, block * columns : (block + 1) * columns] = sums_ref[dst, block].astype(BF16)
    far_out = pltpu.make_async_copy(far_ref, far_hbm.at[0:dst_blocks], out_sems.at[0])
    far_out.start()

    def forward(tile, dst, src):
        total_ref[dst] += dot(adjacency_ref[tile], blocks_ref[src])

    near.each(near_used, GROUP_TILES, forward)
    total_out = pltpu.make_async_copy(total_ref.at[0:dst_blocks], total_hbm.at[0:dst_blocks], out_sems.at[1])
    total_out.start()
    far_out.wait()
    total_out.wait()


def rest_kernel(
    dst_ref, src_ref, count_ref, owner_ref,
    arrived_ref, total_hbm, far_hbm, features_ref, w_self_ref, w_neigh_ref, cotangent_ref, adjacency_hbm,
    output_hbm, partial_ref, message_ref, keep_ref,
    halo_ref, hubs_ref, output_ref, total_ref, far_ref, rows_ref, low_rows_ref, grad_t_ref, source_t_ref,
    back_ref, adjacency_ref, list_ref, counter_ref, tile_sems, sems,
    *, partitions, slots, columns,
):
    me = lax.axis_index("dom")
    tile_rows = adjacency_ref.shape[1]
    dst_blocks = total_ref.shape[0]
    halo_blocks = -(-partitions * slots // tile_rows)
    hub_base = halo_blocks * columns
    total_in = pltpu.make_async_copy(total_hbm.at[0:dst_blocks], total_ref, sems.at[0])
    total_in.start()
    far_in = pltpu.make_async_copy(far_hbm.at[0:dst_blocks], far_ref, sems.at[1])
    far_in.start()

    near = Tiles(list_ref, adjacency_hbm, adjacency_ref, tile_sems)

    def find_near(tile, used):
        code = pack_tile(tile, dst_ref[tile], src_ref[tile])
        list_ref[used] = code
        is_near = code < (dst_blocks << 16)

        @pl.when(is_near)
        def _():
            near.copy(tile).start()

        return used + is_near.astype(jnp.int32)

    used = lax.fori_loop(0, count_ref[0], find_near, jnp.int32(0))
    pad_list(list_ref, used, dst_blocks, dst_blocks, GROUP_TILES)

    rows_ref[...] = jnp.zeros_like(rows_ref)

    def halo_in(q, carry):
        rows_ref[pl.ds(q * slots, slots), :] = arrived_ref[q, 0:slots, :]
        return carry

    repeat(partitions, halo_in, 0)

    def hub_in(hub, owner, slot):
        rows_ref[pl.ds(hub_base + hub, 1), :] = arrived_ref[owner, pl.ds(slots + slot, 1), :]

    hub_slots(owner_ref, counter_ref, partitions, hub_in)
    low_rows = rows_ref[...].astype(BF16)
    low_rows_ref[...] = low_rows
    far_projected = dot(low_rows, w_neigh_ref[...]).astype(BF16)
    total_in.wait()
    far_in.wait()

    root = 0.7978845608028654
    bias_sum = jnp.zeros((1, output_ref.shape[1]), F32)
    w_self_t = jnp.zeros((output_ref.shape[1], features_ref.shape[1]), F32)
    far_t = jnp.zeros((output_ref.shape[1], far_ref.shape[2]), F32)
    for block in range(dst_blocks):
        span = slice(block * tile_rows, (block + 1) * tile_rows)
        v = total_ref[block] + dot(far_ref[block], far_projected)
        square = v * v
        gate = jnp.tanh(root * (v + 0.044715 * (v * square)))
        half = 0.5 * (1.0 + gate)
        output_ref[span, :] = (v * half).astype(BF16)
        slope = half + (0.5 * root) * v * (1.0 - gate * gate) * (1.0 + (3 * 0.044715) * square)
        grad = cotangent_ref[span, :].astype(F32) * slope
        bias_sum += jnp.sum(grad, axis=0, keepdims=True)
        low_t = jnp.transpose(grad.astype(BF16))
        grad_t_ref[block] = low_t
        partial_ref[span, :] = dot_nt(grad.astype(BF16), w_self_ref[...])
        w_self_t += dot(low_t, features_ref[span, :])
        far_t += dot(low_t, far_ref[block])
    output_out = pltpu.make_async_copy(output_ref, output_hbm, sems.at[2])
    output_out.start()
    grad_t_ref[dst_blocks] = jnp.zeros(grad_t_ref.shape[1:], BF16)
    source_t_ref[...] = jnp.zeros_like(source_t_ref)

    def backward(tile, dst, src):
        source_t_ref[src] += dot(grad_t_ref[dst], adjacency_ref[tile])

    near.each(used, GROUP_TILES, backward)

    back_ref[...] = dot_nt(jnp.transpose(far_t.astype(BF16)), w_neigh_ref[...])
    w_neigh_t = dot(far_t.astype(BF16), low_rows_ref[...])
    for block in range(dst_blocks):
        span = slice(block * tile_rows, (block + 1) * tile_rows)
        source_t = source_t_ref[block].astype(BF16)
        w_neigh_t += dot(source_t, features_ref[span, :])
        partial_ref[span, :] += dot_nt(jnp.transpose(source_t), w_neigh_ref[...])

    def halo_out(q, carry):
        halo_ref[pl.ds((q ^ me) * slots, slots), :] = back_ref[pl.ds(q * slots, slots), :]
        return carry

    repeat(partitions, halo_out, 0)
    hubs_ref[...] = jnp.zeros_like(hubs_ref)

    def hub_out(hub, owner, slot):
        hubs_ref[pl.ds((owner ^ me) * HUB_MOST + slot, 1), :] = back_ref[pl.ds(hub_base + hub, 1), :]

    hub_slots(owner_ref, counter_ref, partitions, hub_out)
    plan = Exchange(partitions, slots, 0)
    message_ref[0 : plan.weights, :] = jnp.concatenate([w_self_t, w_neigh_t], axis=0).astype(BF16)
    plan.write(message_ref, keep_ref, halo_ref[...], hubs_ref[...], bias_sum)
    output_out.wait()


class Exchange:
    weights = 256

    def __init__(self, partitions, slots, step):
        self.groups = 1 << step
        self.half = partitions >> (step + 1)
        self.slots = slots
        self.halo = self.groups * self.half * slots
        self.hub = self.half * HUB_MOST
        self.keep = self.halo + self.hub
        self.rows = self.weights + -(-(self.keep + 2) // 16) * 16

    def halves(self, rows, width):
        lower, upper = [], []
        span = self.half * width
        for group in range(rows.shape[0] // (2 * span)):
            base = 2 * group * span
            lower.append(rows[base : base + span])
            upper.append(rows[base + span : base + 2 * span])
        return lower, upper

    def write(self, message_ref, keep_ref, halo, hubs, bias):
        halo_keep, halo_send = self.halves(halo, self.slots)
        hub_keep, hub_send = self.halves(hubs, HUB_MOST)
        high = bias.astype(BF16).astype(F32)
        spare = self.rows - self.weights - self.keep - 2
        parts = halo_send + hub_send + [high, bias - high]
        if spare:
            parts.append(jnp.zeros((spare, bias.shape[1]), F32))
        sent = jnp.concatenate(parts, axis=0).astype(BF16)
        message_ref[self.weights : self.rows, :] = sent
        keep_ref[...] = jnp.concatenate(halo_keep + hub_keep, axis=0)
        return sent

    def tail(self, ref):
        return ref[self.weights : self.rows, :].astype(F32)

    def bias(self, own, other):
        k = self.keep
        return (own[k : k + 1] + own[k + 1 : k + 2]) + (other[k : k + 1] + other[k + 1 : k + 2])

    def merged(self, keep, other):
        halo = jnp.concatenate([keep[: self.halo], other[: self.halo]], axis=0)
        return halo, keep[self.halo :] + other[self.halo : self.keep]

    def weight_sum(self, sent_ref, got_ref):
        rows = slice(0, self.weights)
        return sent_ref[rows, :].astype(F32) + got_ref[rows, :].astype(F32)


def step_kernel(sent_ref, got_ref, keep_ref, message_ref, next_keep_ref, *tail_refs, now, then):
    message_ref[0 : now.weights, :] = now.weight_sum(sent_ref, got_ref).astype(BF16)
    other = now.tail(got_ref)
    halo, hubs = now.merged(keep_ref[...], other)
    sent = then.write(message_ref, next_keep_ref, halo, hubs, now.bias(now.tail(sent_ref), other))
    for tail_ref in tail_refs:
        tail_ref[...] = sent


def prepare_kernel(
    rows_ref, count_ref, owner_ref, hub_row_ref, partial_ref, other_partial_ref, total_ref, target_ref
):
    me = lax.axis_index("dom")
    slots, partitions = rows_ref.shape
    nodes = partial_ref.shape[0]
    steps = partitions.bit_length() - 1
    total_ref[...] = partial_ref[...] + other_partial_ref[...]
    for group in range(partitions):
        origin = me ^ sum(((group >> k) & 1) << (steps - 1 - k) for k in range(steps))
        for slot in range(slots):
            sent = slot < count_ref[origin]
            target_ref[group * slots + slot] = jnp.where(sent, rows_ref[slot, origin], nodes)
    base = partitions * slots
    for slot in range(HUB_MOST):
        target_ref[base + slot] = nodes

    def hub(index, slot):
        mine = (owner_ref[index] == me).astype(jnp.int32)
        target_ref[base + slot] = jnp.where(mine == 1, hub_row_ref[index], nodes)
        return slot + mine

    repeat(owner_ref.shape[0], hub, jnp.int32(0))


def final_kernel(
    target_ref, sent_ref, got_ref, cross_ref, keep_ref, other_keep_ref, total_in_ref,
    w_self_ref, w_neigh_ref, bias_ref, low_ref, total_ref, *, now,
):
    nodes = total_in_ref.shape[0]
    total_ref[0:nodes, :] = total_in_ref[...]
    got = now.tail(got_ref)
    keep = keep_ref[...] + other_keep_ref[...]
    halo, hubs = now.merged(keep, got + cross_ref[...].astype(F32))
    returned = jnp.concatenate([halo, hubs], axis=0)
    for place in range(returned.shape[0]):
        row = pl.ds(target_ref[place], 1)
        total_ref[row, :] += returned[place : place + 1, :]
    low_ref[...] = total_ref[0:nodes, :].astype(BF16)
    weights = now.weight_sum(sent_ref, got_ref)
    split = now.weights // 2
    w_self_ref[...] = jnp.transpose(weights[:split])
    w_neigh_ref[...] = jnp.transpose(weights[split:])
    bias_ref[...] = now.bias(now.tail(sent_ref), got)


SMEM = pl.BlockSpec(memory_space=pltpu.SMEM)
VMEM = pl.BlockSpec(memory_space=pltpu.VMEM)
HBM = pl.BlockSpec(memory_space=pltpu.HBM)


def call(kernel, name, ins, outs, scratch, args, grant, flops=0, size=0, out_specs=None):
    return pl.pallas_call(
        kernel,
        out_shape=outs,
        in_specs=ins,
        out_specs=jax.tree.map(lambda _: VMEM, outs) if out_specs is None else out_specs,
        scratch_shapes=scratch,
        compiler_params=pltpu.CompilerParams(vmem_limit_bytes=grant * 1024 * 1024),
        cost_estimate=pl.CostEstimate(flops=flops, bytes_accessed=size, transcendentals=0),
        name=name,
    )(*args)


def local(
    features, w_self, w_neigh, bias, cotangent, adjacency, tile_dst, tile_src, tile_count,
    send_rows, send_count, hub_owner, hub_row,
):
    nodes, inputs = features.shape
    limit, tile_rows, _ = adjacency.shape
    hidden = w_neigh.shape[1]
    partitions = lax.axis_size("dom")
    slots = send_rows.shape[2]
    hubs = hub_row.shape[0]
    dst_blocks = nodes // tile_rows
    far_blocks = -(-partitions * slots // tile_rows) - (-hubs // tile_rows)
    columns = min(tile_rows, -(-max(partitions * slots, hubs) // 128) * 128)
    rows = jnp.transpose(send_rows[0])
    counts = send_count.reshape(partitions)
    owner = hub_owner.reshape(hubs)
    struct = jax.ShapeDtypeStruct
    lists = pltpu.SMEM((limit + GROUP_TILES,), jnp.int32)

    bundle = call(
        gather_kernel, "gather", [HBM] * 5,
        struct((partitions, PEER_ROWS, inputs), F32),
        [
            pltpu.SMEM((slots, partitions), jnp.int32),
            pltpu.SMEM((partitions,), jnp.int32),
            pltpu.SMEM((hubs,), jnp.int32),
            pltpu.SMEM((hubs,), jnp.int32),
            pltpu.VMEM((nodes, inputs), BF16),
            pltpu.VMEM((nodes, inputs), F32),
            pltpu.VMEM((PEER_ROWS, inputs), F32),
            pltpu.SemaphoreType.DMA((5,)),
        ],
        (rows, counts, owner, hub_row, features), 60,
    )
    arrived = lax.all_to_all(bundle, "dom", split_axis=0, concat_axis=0, tiled=True)
    total, far = call(
        own_kernel, "own_tiles", [HBM] * 8,
        (
            struct((limit, tile_rows, hidden), F32),
            struct((limit, tile_rows, far_blocks * columns), BF16),
        ),
        [
            pltpu.SMEM((limit,), jnp.int32),
            pltpu.SMEM((limit,), jnp.int32),
            pltpu.SMEM((1,), jnp.int32),
            pltpu.VMEM((nodes, inputs), BF16),
            pltpu.VMEM((inputs, hidden), BF16),
            pltpu.VMEM((inputs, hidden), BF16),
            pltpu.VMEM((1, hidden), F32),
            pltpu.VMEM(adjacency.shape, BF16),
            pltpu.VMEM((dst_blocks + 1, tile_rows, hidden), BF16),
            pltpu.VMEM((dst_blocks + 1, tile_rows, hidden), F32),
            pltpu.VMEM((dst_blocks + 1, far_blocks, tile_rows, columns), F32),
            pltpu.VMEM((dst_blocks, tile_rows, far_blocks * columns), BF16),
            lists,
            lists,
            pltpu.SemaphoreType.DMA((7,)),
            pltpu.SemaphoreType.DMA((limit,)),
            pltpu.SemaphoreType.DMA((2,)),
        ],
        (tile_dst, tile_src, tile_count, features, w_self, w_neigh, bias.reshape(1, hidden), adjacency),
        54, flops=2 * limit * tile_rows * tile_rows * hidden, size=adjacency.size * 2, out_specs=(HBM, HBM),
    )
    plans = [Exchange(partitions, slots, step) for step in range(partitions.bit_length() - 1)]
    output, partial, message, keep = call(
        functools.partial(rest_kernel, partitions=partitions, slots=slots, columns=columns), "rest",
        [SMEM] * 4 + [VMEM, HBM, HBM] + [VMEM] * 4 + [HBM],
        (
            struct((nodes, hidden), BF16),
            struct((nodes, inputs), F32),
            struct((plans[0].rows, inputs), BF16),
            struct((plans[0].keep, inputs), F32),
        ),
        [
            pltpu.VMEM((partitions * slots, inputs), F32),
            pltpu.VMEM((partitions * HUB_MOST, inputs), F32),
            pltpu.VMEM((nodes, hidden), BF16),
            pltpu.VMEM((dst_blocks, tile_rows, hidden), F32),
            pltpu.VMEM((dst_blocks, tile_rows, far_blocks * columns), BF16),
            pltpu.VMEM((far_blocks * columns, inputs), F32),
            pltpu.VMEM((far_blocks * columns, inputs), BF16),
            pltpu.VMEM((dst_blocks + 1, hidden, tile_rows), BF16),
            pltpu.VMEM((dst_blocks + 1, hidden, tile_rows), F32),
            pltpu.VMEM((far_blocks * columns, inputs), F32),
            pltpu.VMEM(adjacency.shape, BF16),
            lists,
            pltpu.SMEM((partitions,), jnp.int32),
            pltpu.SemaphoreType.DMA((limit,)),
            pltpu.SemaphoreType.DMA((3,)),
        ],
        (
            tile_dst, tile_src, tile_count, owner,
            arrived, total, far, features, w_self, w_neigh, cotangent, adjacency,
        ),
        50, out_specs=(HBM, VMEM, VMEM, VMEM),
    )
    swap = [(0, 1), (1, 0)]
    tail = None
    for now, then in zip(plans, plans[1:]):
        got = lax.ppermute(message, "dom", [(q, q ^ now.half) for q in range(partitions)])
        if now is plans[0]:
            got, late_partial = lax.optimization_barrier((got, partial))
        outs = [struct((then.rows, inputs), BF16), struct((then.keep, inputs), F32)]
        if then is plans[-1]:
            outs.append(struct((then.rows - then.weights, inputs), BF16))
        message, keep, *tail = call(
            functools.partial(step_kernel, now=now, then=then), "step", [VMEM] * 3,
            tuple(outs), [], (message, got, keep), 16,
        )
    now = plans[-1]
    got = lax.ppermute(message, "dom", [(q, q ^ 1) for q in range(partitions)])
    cross = lax.ppermute(tail[0], ("dom", "feat"), [(k, k ^ 3) for k in range(2 * partitions)])
    other_keep = lax.ppermute(keep, "feat", swap)
    other_partial = lax.ppermute(late_partial, "feat", swap)
    summed, target = call(
        prepare_kernel, "prepare", [SMEM] * 4 + [VMEM] * 2,
        (struct((nodes, inputs), F32), struct((partitions * slots + HUB_MOST,), jnp.int32)),
        [], (rows, counts, owner, hub_row, partial, other_partial), 16,
        flops=10**6, size=4 * 10**6, out_specs=(VMEM, SMEM),
    )
    grad_w_self, grad_w_neigh, grad_bias, grad_features = call(
        functools.partial(final_kernel, now=now), "final", [SMEM] + [VMEM] * 6,
        (
            struct((inputs, hidden), F32), struct((inputs, hidden), F32), struct((1, hidden), F32),
            struct((nodes, inputs), BF16),
        ),
        [pltpu.VMEM((nodes + 8, inputs), F32)],
        (target, message, got, cross, keep, other_keep, summed), 32,
    )
    return (output, grad_features, grad_w_self, grad_w_neigh, grad_bias.reshape(hidden))


def solution(mesh):
    return jax.shard_map(
        local,
        mesh=mesh,
        in_specs=(
            P(("group", "dom"), None),
            P(None, "feat"),
            P(None, "feat"),
            P("feat"),
            P(("group", "dom"), "feat"),
            P(("group", "dom"), None, None),
            P(("group", "dom")),
            P(("group", "dom")),
            P(("group", "dom")),
            P(("group", "dom"), None, None),
            P(("group", "dom"), None),
            P("group", None),
            P("group"),
        ),
        out_specs=(
            P(("group", "dom"), "feat"),
            P(("group", "dom"), None),
            P("group", "feat"),
            P("group", "feat"),
            P(("group", "feat")),
        ),
        check_vma=False,
    )
```

```python
import functools

import jax
import jax.numpy as jnp
from jax import lax
from jax.experimental import pallas as pl
from jax.experimental.pallas import tpu as pltpu
from jax.sharding import PartitionSpec as P

HUB_MOST = 4
PEER_ROWS = 8
GROUP_TILES = 8
FAR_GROUP = 4
F32 = jnp.float32
BF16 = jnp.bfloat16
NT = (((1,), (1,)), ((), ()))


def dot(a, b):
    return jnp.dot(a, b, preferred_element_type=F32)


def dot_nt(a, b):
    return lax.dot_general(a, b, NT, preferred_element_type=F32)


def repeat(count, body, init):
    return lax.fori_loop(0, count, body, init, unroll=True)


def hub_slots(owner_ref, counter_ref, partitions, body):
    def clear(q, carry):
        counter_ref[q] = 0
        return carry

    def visit(hub, carry):
        owner = owner_ref[hub]
        slot = counter_ref[owner]
        counter_ref[owner] = slot + 1
        body(hub, owner, slot)
        return carry

    repeat(partitions, clear, 0)
    repeat(owner_ref.shape[0], visit, 0)


def fetch(pairs, sems):
    copies = [pltpu.make_async_copy(src, dst, sems.at[k]) for k, (src, dst) in enumerate(pairs)]
    for copy in copies:
        copy.start()
    return copies


def gather_kernel(
    rows_hbm, count_hbm, owner_hbm, hub_row_hbm, features_hbm,
    bundle_ref,
    rows_ref, count_ref, owner_ref, hub_row_ref, features_ref, wide_ref, hubs_ref, sems,
):
    own = lax.axis_index("dom")
    partitions = bundle_ref.shape[0]
    slots = rows_ref.shape[0]
    copies = fetch(
        [
            (features_hbm, features_ref), (rows_hbm, rows_ref), (count_hbm, count_ref),
            (owner_hbm, owner_ref), (hub_row_hbm, hub_row_ref),
        ],
        sems,
    )
    hubs_ref[...] = jnp.zeros_like(hubs_ref)
    for copy in copies:
        copy.wait()
    wide_ref[...] = features_ref[...].astype(F32)

    def hub(index, slot):
        hubs_ref[pl.ds(slots + slot, 1), :] = wide_ref[pl.ds(hub_row_ref[index], 1), :]
        return slot + (owner_ref[index] == own).astype(jnp.int32)

    repeat(owner_ref.shape[0], hub, jnp.int32(0))

    def peer(q, carry):
        bundle_ref[q] = hubs_ref[...]
        for slot in range(slots):
            row = wide_ref[pl.ds(rows_ref[slot, q], 1), :]
            bundle_ref[q, slot : slot + 1, :] = jnp.where(slot < count_ref[q], row, 0.0)
        return carry

    repeat(partitions, peer, 0)


def pack_tile(tile, dst, src):
    return tile + (dst << 8) + (src << 16)


def pad_list(list_ref, used, dst, src, group):
    spare = pack_tile(list_ref[0] & 255, dst, src)
    for k in range(group):
        list_ref[used + k] = spare


class Tiles:
    def __init__(self, list_ref, source, held, sems, columns=None):
        self.list_ref, self.source, self.held, self.sems = list_ref, source, held, sems
        self.columns = held.shape[2] if columns is None else columns

    def copy(self, tile):
        span = slice(0, self.columns)
        return pltpu.make_async_copy(
            self.source.at[tile, :, span], self.held.at[tile, :, span], self.sems.at[tile]
        )

    def start(self, total):
        def one(position, carry):
            self.copy(self.list_ref[position] & 255).start()
            return carry

        lax.fori_loop(0, total, one, 0)

    def each(self, total, size, body):
        def group(step, carry):
            codes = [self.list_ref[step * size + k] for k in range(size)]
            for k in range(size):

                @pl.when(step * size + k < total)
                def _(k=k):
                    self.copy(codes[k] & 255).wait()

            for code in codes:
                body(code & 255, (code >> 8) & 255, code >> 16)
            return carry

        lax.fori_loop(0, (total + size - 1) // size, group, 0)


def own_kernel(
    dst_hbm, src_hbm, count_hbm, features_hbm, w_self_hbm, w_neigh_hbm, bias_hbm, adjacency_hbm,
    total_hbm, far_hbm,
    dst_ref, src_ref, count_ref, features_ref, w_self_ref, w_neigh_ref, bias_ref,
    adjacency_ref, blocks_ref, total_ref, sums_ref, far_ref, list_ref, far_list_ref, sems, tile_sems, out_sems,
):
    tile_rows = adjacency_ref.shape[1]
    dst_blocks = total_ref.shape[0] - 1
    far_blocks, columns = sums_ref.shape[1], sums_ref.shape[3]
    copies = fetch(
        [
            (src_hbm, src_ref), (dst_hbm, dst_ref), (count_hbm, count_ref), (w_neigh_hbm, w_neigh_ref),
            (features_hbm, features_ref), (w_self_hbm, w_self_ref), (bias_hbm, bias_ref),
        ],
        sems,
    )
    sums_ref[...] = jnp.zeros_like(sums_ref)
    for copy in copies[:3]:
        copy.wait()
    far = Tiles(far_list_ref, adjacency_hbm, adjacency_ref, tile_sems, columns)
    near = Tiles(list_ref, adjacency_hbm, adjacency_ref, tile_sems)

    def split(tile, used):
        near_used, far_used = used
        code = pack_tile(tile, dst_ref[tile], src_ref[tile])
        list_ref[near_used] = code
        far_list_ref[far_used] = code
        is_near = (code < (dst_blocks << 16)).astype(jnp.int32)

        @pl.when(is_near == 0)
        def _():
            far.copy(tile).start()

        return near_used + is_near, far_used + 1 - is_near

    near_used, far_used = lax.fori_loop(0, count_ref[0], split, (jnp.int32(0), jnp.int32(0)))
    near.start(near_used)
    pad_list(list_ref, near_used, dst_blocks, dst_blocks, GROUP_TILES)
    pad_list(far_list_ref, far_used, dst_blocks, dst_blocks, FAR_GROUP)
    for copy in copies[3:]:
        copy.wait()
    features = features_ref[...]
    projected = dot(features, w_neigh_ref[...]).astype(BF16)
    for block in range(dst_blocks):
        blocks_ref[block] = projected[block * tile_rows : (block + 1) * tile_rows]
    blocks_ref[dst_blocks] = jnp.zeros(blocks_ref.shape[1:], BF16)
    base = dot(features, w_self_ref[...]) + bias_ref[...]
    for block in range(dst_blocks):
        total_ref[block] = base[block * tile_rows : (block + 1) * tile_rows]
    total_ref[dst_blocks] = jnp.zeros(total_ref.shape[1:], F32)

    def add_far(tile, dst, src):
        sums_ref[dst, src - dst_blocks] += adjacency_ref[tile, :, :columns].astype(F32)

    far.each(far_used, FAR_GROUP, add_far)
    for dst in range(dst_blocks):
        for block in range(far_blocks):
            far_ref[dst, :, block * columns : (block + 1) * columns] = sums_ref[dst, block].astype(BF16)
    far_out = pltpu.make_async_copy(far_ref, far_hbm.at[0:dst_blocks], out_sems.at[0])
    far_out.start()

    def forward(tile, dst, src):
        total_ref[dst] += dot(adjacency_ref[tile], blocks_ref[src])

    near.each(near_used, GROUP_TILES, forward)
    total_out = pltpu.make_async_copy(total_ref.at[0:dst_blocks], total_hbm.at[0:dst_blocks], out_sems.at[1])
    total_out.start()
    far_out.wait()
    total_out.wait()


def rest_kernel(
    dst_hbm, src_hbm, count_hbm, owner_hbm,
    arrived_ref, total_hbm, far_hbm, features_ref, w_self_ref, w_neigh_ref, cotangent_ref, adjacency_hbm,
    output_hbm, partial_ref, message_ref, keep_ref,
    halo_ref, hubs_ref, output_ref, total_ref, far_ref, rows_ref, low_rows_ref, grad_t_ref, source_t_ref,
    back_ref, adjacency_ref, list_ref, counter_ref, dst_ref, src_ref, count_ref, owner_ref, tile_sems, sems, scalar_sems,
    *, partitions, slots, columns,
):
    me = lax.axis_index("dom")
    tile_rows = adjacency_ref.shape[1]
    dst_blocks = total_ref.shape[0]
    halo_blocks = -(-partitions * slots // tile_rows)
    hub_base = halo_blocks * columns
    scalars = fetch(
        [(src_hbm, src_ref), (dst_hbm, dst_ref), (count_hbm, count_ref), (owner_hbm, owner_ref)], scalar_sems
    )
    total_in = pltpu.make_async_copy(total_hbm.at[0:dst_blocks], total_ref, sems.at[0])
    total_in.start()
    far_in = pltpu.make_async_copy(far_hbm.at[0:dst_blocks], far_ref, sems.at[1])
    far_in.start()
    rows_ref[...] = jnp.zeros_like(rows_ref)
    source_t_ref[...] = jnp.zeros_like(source_t_ref)
    grad_t_ref[dst_blocks] = jnp.zeros(grad_t_ref.shape[1:], BF16)
    for copy in scalars:
        copy.wait()
    near = Tiles(list_ref, adjacency_hbm, adjacency_ref, tile_sems)

    def find_near(tile, used):
        code = pack_tile(tile, dst_ref[tile], src_ref[tile])
        list_ref[used] = code
        is_near = code < (dst_blocks << 16)

        @pl.when(is_near)
        def _():
            near.copy(tile).start()

        return used + is_near.astype(jnp.int32)

    used = lax.fori_loop(0, count_ref[0], find_near, jnp.int32(0))
    pad_list(list_ref, used, dst_blocks, dst_blocks, GROUP_TILES)

    def halo_in(q, carry):
        rows_ref[pl.ds(q * slots, slots), :] = arrived_ref[q, 0:slots, :]
        return carry

    repeat(partitions, halo_in, 0)

    def hub_in(hub, owner, slot):
        rows_ref[pl.ds(hub_base + hub, 1), :] = arrived_ref[owner, pl.ds(slots + slot, 1), :]

    hub_slots(owner_ref, counter_ref, partitions, hub_in)
    low_rows = rows_ref[...].astype(BF16)
    low_rows_ref[...] = low_rows
    far_projected = dot(low_rows, w_neigh_ref[...]).astype(BF16)
    total_in.wait()
    far_in.wait()

    root = 0.7978845608028654
    bias_sum = jnp.zeros((1, output_ref.shape[1]), F32)
    w_self_t = jnp.zeros((output_ref.shape[1], features_ref.shape[1]), F32)
    far_t = jnp.zeros((output_ref.shape[1], far_ref.shape[2]), F32)
    for block in range(dst_blocks):
        span = slice(block * tile_rows, (block + 1) * tile_rows)
        v = total_ref[block] + dot(far_ref[block], far_projected)
        square = v * v
        gate = jnp.tanh(root * (v + 0.044715 * (v * square)))
        half = 0.5 * (1.0 + gate)
        output_ref[span, :] = (v * half).astype(BF16)
        slope = half + (0.5 * root) * v * (1.0 - gate * gate) * (1.0 + (3 * 0.044715) * square)
        grad = cotangent_ref[span, :].astype(F32) * slope
        bias_sum += jnp.sum(grad, axis=0, keepdims=True)
        low_t = jnp.transpose(grad.astype(BF16))
        grad_t_ref[block] = low_t
        partial_ref[span, :] = dot_nt(grad.astype(BF16), w_self_ref[...])
        w_self_t += dot(low_t, features_ref[span, :])
        far_t += dot(low_t, far_ref[block])
    output_out = pltpu.make_async_copy(output_ref, output_hbm, sems.at[2])
    output_out.start()

    def backward(tile, dst, src):
        source_t_ref[src] += dot(grad_t_ref[dst], adjacency_ref[tile])

    near.each(used, GROUP_TILES, backward)

    back_ref[...] = dot_nt(jnp.transpose(far_t.astype(BF16)), w_neigh_ref[...])
    w_neigh_t = dot(far_t.astype(BF16), low_rows_ref[...])
    for block in range(dst_blocks):
        span = slice(block * tile_rows, (block + 1) * tile_rows)
        source_t = source_t_ref[block].astype(BF16)
        w_neigh_t += dot(source_t, features_ref[span, :])
        partial_ref[span, :] += dot_nt(jnp.transpose(source_t), w_neigh_ref[...])

    def halo_out(q, carry):
        halo_ref[pl.ds((q ^ me) * slots, slots), :] = back_ref[pl.ds(q * slots, slots), :]
        return carry

    repeat(partitions, halo_out, 0)
    hubs_ref[...] = jnp.zeros_like(hubs_ref)

    def hub_out(hub, owner, slot):
        hubs_ref[pl.ds((owner ^ me) * HUB_MOST + slot, 1), :] = back_ref[pl.ds(hub_base + hub, 1), :]

    hub_slots(owner_ref, counter_ref, partitions, hub_out)
    plan = Exchange(partitions, slots, 0)
    message_ref[0 : plan.weights, :] = jnp.concatenate([w_self_t, w_neigh_t], axis=0).astype(BF16)
    plan.write(message_ref, keep_ref, halo_ref[...], hubs_ref[...], bias_sum)
    output_out.wait()


class Exchange:
    weights = 256

    def __init__(self, partitions, slots, step):
        self.groups = 1 << step
        self.half = partitions >> (step + 1)
        self.slots = slots
        self.halo = self.groups * self.half * slots
        self.hub = self.half * HUB_MOST
        self.keep = self.halo + self.hub
        self.rows = self.weights + -(-(self.keep + 2) // 16) * 16

    def halves(self, rows, width):
        lower, upper = [], []
        span = self.half * width
        for group in range(rows.shape[0] // (2 * span)):
            base = 2 * group * span
            lower.append(rows[base : base + span])
            upper.append(rows[base + span : base + 2 * span])
        return lower, upper

    def write(self, message_ref, keep_ref, halo, hubs, bias):
        halo_keep, halo_send = self.halves(halo, self.slots)
        hub_keep, hub_send = self.halves(hubs, HUB_MOST)
        high = bias.astype(BF16).astype(F32)
        spare = self.rows - self.weights - self.keep - 2
        parts = halo_send + hub_send + [high, bias - high]
        if spare:
            parts.append(jnp.zeros((spare, bias.shape[1]), F32))
        sent = jnp.concatenate(parts, axis=0).astype(BF16)
        message_ref[self.weights : self.rows, :] = sent
        keep_ref[...] = jnp.concatenate(halo_keep + hub_keep, axis=0)
        return sent

    def tail(self, ref):
        return ref[self.weights : self.rows, :].astype(F32)

    def bias(self, own, other):
        k = self.keep
        return (own[k : k + 1] + own[k + 1 : k + 2]) + (other[k : k + 1] + other[k + 1 : k + 2])

    def merged(self, keep, other):
        halo = jnp.concatenate([keep[: self.halo], other[: self.halo]], axis=0)
        return halo, keep[self.halo :] + other[self.halo : self.keep]

    def weight_sum(self, sent_ref, got_ref):
        rows = slice(0, self.weights)
        return sent_ref[rows, :].astype(F32) + got_ref[rows, :].astype(F32)


def step_kernel(sent_ref, got_ref, keep_ref, message_ref, next_keep_ref, *tail_refs, now, then):
    message_ref[0 : now.weights, :] = now.weight_sum(sent_ref, got_ref).astype(BF16)
    other = now.tail(got_ref)
    halo, hubs = now.merged(keep_ref[...], other)
    sent = then.write(message_ref, next_keep_ref, halo, hubs, now.bias(now.tail(sent_ref), other))
    for tail_ref in tail_refs:
        tail_ref[...] = sent


def prepare_kernel(
    rows_ref, count_ref, owner_ref, hub_row_ref, partial_ref, other_partial_ref, total_ref, target_ref
):
    me = lax.axis_index("dom")
    slots, partitions = rows_ref.shape
    nodes = partial_ref.shape[0]
    steps = partitions.bit_length() - 1
    total_ref[...] = partial_ref[...] + other_partial_ref[...]
    for group in range(partitions):
        origin = me ^ sum(((group >> k) & 1) << (steps - 1 - k) for k in range(steps))
        for slot in range(slots):
            sent = slot < count_ref[origin]
            target_ref[group * slots + slot] = jnp.where(sent, rows_ref[slot, origin], nodes)
    base = partitions * slots
    for slot in range(HUB_MOST):
        target_ref[base + slot] = nodes

    def hub(index, slot):
        mine = (owner_ref[index] == me).astype(jnp.int32)
        target_ref[base + slot] = jnp.where(mine == 1, hub_row_ref[index], nodes)
        return slot + mine

    repeat(owner_ref.shape[0], hub, jnp.int32(0))


def final_kernel(
    target_hbm, sent_ref, got_ref, cross_ref, keep_ref, other_keep_ref, total_in_ref,
    w_self_ref, w_neigh_ref, bias_ref, low_ref, total_ref, target_ref, sem, *, now,
):
    nodes = total_in_ref.shape[0]
    target_in = pltpu.make_async_copy(target_hbm, target_ref, sem)
    target_in.start()
    total_ref[0:nodes, :] = total_in_ref[...]
    got = now.tail(got_ref)
    keep = keep_ref[...] + other_keep_ref[...]
    halo, hubs = now.merged(keep, got + cross_ref[...].astype(F32))
    returned = jnp.concatenate([halo, hubs], axis=0)
    target_in.wait()
    for place in range(returned.shape[0]):
        row = pl.ds(target_ref[place], 1)
        total_ref[row, :] += returned[place : place + 1, :]
    low_ref[...] = total_ref[0:nodes, :].astype(BF16)
    weights = now.weight_sum(sent_ref, got_ref)
    split = now.weights // 2
    w_self_ref[...] = jnp.transpose(weights[:split])
    w_neigh_ref[...] = jnp.transpose(weights[split:])
    bias_ref[...] = now.bias(now.tail(sent_ref), got)


SMEM = pl.BlockSpec(memory_space=pltpu.SMEM)
VMEM = pl.BlockSpec(memory_space=pltpu.VMEM)
HBM = pl.BlockSpec(memory_space=pltpu.HBM)


def call(kernel, name, ins, outs, scratch, args, grant, flops=0, size=0, out_specs=None):
    return pl.pallas_call(
        kernel,
        out_shape=outs,
        in_specs=ins,
        out_specs=jax.tree.map(lambda _: VMEM, outs) if out_specs is None else out_specs,
        scratch_shapes=scratch,
        compiler_params=pltpu.CompilerParams(vmem_limit_bytes=grant * 1024 * 1024),
        cost_estimate=pl.CostEstimate(flops=flops, bytes_accessed=size, transcendentals=0),
        name=name,
    )(*args)


def local(
    features, w_self, w_neigh, bias, cotangent, adjacency, tile_dst, tile_src, tile_count,
    send_rows, send_count, hub_owner, hub_row,
):
    nodes, inputs = features.shape
    limit, tile_rows, _ = adjacency.shape
    hidden = w_neigh.shape[1]
    partitions = lax.axis_size("dom")
    slots = send_rows.shape[2]
    hubs = hub_row.shape[0]
    dst_blocks = nodes // tile_rows
    far_blocks = -(-partitions * slots // tile_rows) - (-hubs // tile_rows)
    columns = min(tile_rows, -(-max(partitions * slots, hubs) // 128) * 128)
    rows = jnp.transpose(send_rows[0])
    counts = send_count.reshape(partitions)
    owner = hub_owner.reshape(hubs)
    struct = jax.ShapeDtypeStruct
    lists = pltpu.SMEM((limit + GROUP_TILES,), jnp.int32)

    bundle = call(
        gather_kernel, "gather", [HBM] * 5,
        struct((partitions, PEER_ROWS, inputs), F32),
        [
            pltpu.SMEM((slots, partitions), jnp.int32),
            pltpu.SMEM((partitions,), jnp.int32),
            pltpu.SMEM((hubs,), jnp.int32),
            pltpu.SMEM((hubs,), jnp.int32),
            pltpu.VMEM((nodes, inputs), BF16),
            pltpu.VMEM((nodes, inputs), F32),
            pltpu.VMEM((PEER_ROWS, inputs), F32),
            pltpu.SemaphoreType.DMA((5,)),
        ],
        (rows, counts, owner, hub_row, features), 60,
    )
    arrived = lax.all_to_all(bundle, "dom", split_axis=0, concat_axis=0, tiled=True)
    total, far = call(
        own_kernel, "own_tiles", [HBM] * 8,
        (
            struct((limit, tile_rows, hidden), F32),
            struct((limit, tile_rows, far_blocks * columns), BF16),
        ),
        [
            pltpu.SMEM((limit,), jnp.int32),
            pltpu.SMEM((limit,), jnp.int32),
            pltpu.SMEM((1,), jnp.int32),
            pltpu.VMEM((nodes, inputs), BF16),
            pltpu.VMEM((inputs, hidden), BF16),
            pltpu.VMEM((inputs, hidden), BF16),
            pltpu.VMEM((1, hidden), F32),
            pltpu.VMEM(adjacency.shape, BF16),
            pltpu.VMEM((dst_blocks + 1, tile_rows, hidden), BF16),
            pltpu.VMEM((dst_blocks + 1, tile_rows, hidden), F32),
            pltpu.VMEM((dst_blocks + 1, far_blocks, tile_rows, columns), F32),
            pltpu.VMEM((dst_blocks, tile_rows, far_blocks * columns), BF16),
            lists,
            lists,
            pltpu.SemaphoreType.DMA((7,)),
            pltpu.SemaphoreType.DMA((limit,)),
            pltpu.SemaphoreType.DMA((2,)),
        ],
        (tile_dst, tile_src, tile_count, features, w_self, w_neigh, bias.reshape(1, hidden), adjacency),
        54, flops=2 * limit * tile_rows * tile_rows * hidden, size=adjacency.size * 2, out_specs=(HBM, HBM),
    )
    plans = [Exchange(partitions, slots, step) for step in range(partitions.bit_length() - 1)]
    output, partial, message, keep = call(
        functools.partial(rest_kernel, partitions=partitions, slots=slots, columns=columns), "rest",
        [HBM] * 4 + [VMEM, HBM, HBM] + [VMEM] * 4 + [HBM],
        (
            struct((nodes, hidden), BF16),
            struct((nodes, inputs), F32),
            struct((plans[0].rows, inputs), BF16),
            struct((plans[0].keep, inputs), F32),
        ),
        [
            pltpu.VMEM((partitions * slots, inputs), F32),
            pltpu.VMEM((partitions * HUB_MOST, inputs), F32),
            pltpu.VMEM((nodes, hidden), BF16),
            pltpu.VMEM((dst_blocks, tile_rows, hidden), F32),
            pltpu.VMEM((dst_blocks, tile_rows, far_blocks * columns), BF16),
            pltpu.VMEM((far_blocks * columns, inputs), F32),
            pltpu.VMEM((far_blocks * columns, inputs), BF16),
            pltpu.VMEM((dst_blocks + 1, hidden, tile_rows), BF16),
            pltpu.VMEM((dst_blocks + 1, hidden, tile_rows), F32),
            pltpu.VMEM((far_blocks * columns, inputs), F32),
            pltpu.VMEM(adjacency.shape, BF16),
            lists,
            pltpu.SMEM((partitions,), jnp.int32),
            pltpu.SMEM((limit,), jnp.int32),
            pltpu.SMEM((limit,), jnp.int32),
            pltpu.SMEM((1,), jnp.int32),
            pltpu.SMEM((hubs,), jnp.int32),
            pltpu.SemaphoreType.DMA((limit,)),
            pltpu.SemaphoreType.DMA((3,)),
            pltpu.SemaphoreType.DMA((4,)),
        ],
        (
            tile_dst, tile_src, tile_count, owner,
            arrived, total, far, features, w_self, w_neigh, cotangent, adjacency,
        ),
        50, out_specs=(HBM, VMEM, VMEM, VMEM),
    )
    swap = [(0, 1), (1, 0)]
    tail = None
    for now, then in zip(plans, plans[1:]):
        got = lax.ppermute(message, "dom", [(q, q ^ now.half) for q in range(partitions)])
        if now is plans[0]:
            got, late_partial = lax.optimization_barrier((got, partial))
        outs = [struct((then.rows, inputs), BF16), struct((then.keep, inputs), F32)]
        if then is plans[-1]:
            outs.append(struct((then.rows - then.weights, inputs), BF16))
        message, keep, *tail = call(
            functools.partial(step_kernel, now=now, then=then), "step", [VMEM] * 3,
            tuple(outs), [], (message, got, keep), 16,
        )
    now = plans[-1]
    got = lax.ppermute(message, "dom", [(q, q ^ 1) for q in range(partitions)])
    cross = lax.ppermute(tail[0], ("dom", "feat"), [(k, k ^ 3) for k in range(2 * partitions)])
    other_keep = lax.ppermute(keep, "feat", swap)
    other_partial = lax.ppermute(late_partial, "feat", swap)
    summed, target = call(
        prepare_kernel, "prepare", [SMEM] * 4 + [VMEM] * 2,
        (struct((nodes, inputs), F32), struct((partitions * slots + HUB_MOST,), jnp.int32)),
        [], (rows, counts, owner, hub_row, partial, other_partial), 16,
        flops=10**6, size=4 * 10**6, out_specs=(VMEM, SMEM),
    )
    grad_w_self, grad_w_neigh, grad_bias, grad_features = call(
        functools.partial(final_kernel, now=now), "final", [HBM] + [VMEM] * 6,
        (
            struct((inputs, hidden), F32), struct((inputs, hidden), F32), struct((1, hidden), F32),
            struct((nodes, inputs), BF16),
        ),
        [
            pltpu.VMEM((nodes + 8, inputs), F32),
            pltpu.SMEM((partitions * slots + HUB_MOST,), jnp.int32),
            pltpu.SemaphoreType.DMA,
        ],
        (target, message, got, cross, keep, other_keep, summed), 32,
    )
    return (output, grad_features, grad_w_self, grad_w_neigh, grad_bias.reshape(hidden))


def solution(mesh):
    return jax.shard_map(
        local,
        mesh=mesh,
        in_specs=(
            P(("group", "dom"), None),
            P(None, "feat"),
            P(None, "feat"),
            P("feat"),
            P(("group", "dom"), "feat"),
            P(("group", "dom"), None, None),
            P(("group", "dom")),
            P(("group", "dom")),
            P(("group", "dom")),
            P(("group", "dom"), None, None),
            P(("group", "dom"), None),
            P("group", None),
            P("group"),
        ),
        out_specs=(
            P(("group", "dom"), "feat"),
            P(("group", "dom"), None),
            P("group", "feat"),
            P("group", "feat"),
            P(("group", "feat")),
        ),
        check_vma=False,
    )
```

```python
import functools

import jax
import jax.numpy as jnp
from jax import lax
from jax.experimental import pallas as pl
from jax.experimental.pallas import tpu as pltpu
from jax.sharding import PartitionSpec as P

HUB_MOST = 4
PEER_ROWS = 8
GROUP_TILES = 8
FAR_GROUP = 4
F32 = jnp.float32
BF16 = jnp.bfloat16
NT = (((1,), (1,)), ((), ()))


def dot(a, b):
    return jnp.dot(a, b, preferred_element_type=F32)


def dot_nt(a, b):
    return lax.dot_general(a, b, NT, preferred_element_type=F32)


def repeat(count, body, init):
    return lax.fori_loop(0, count, body, init, unroll=True)


def hub_slots(owner_ref, counter_ref, partitions, body):
    def clear(q, carry):
        counter_ref[q] = 0
        return carry

    def visit(hub, carry):
        owner = owner_ref[hub]
        slot = counter_ref[owner]
        counter_ref[owner] = slot + 1
        body(hub, owner, slot)
        return carry

    repeat(partitions, clear, 0)
    repeat(owner_ref.shape[0], visit, 0)


def fetch(pairs, sems):
    copies = [pltpu.make_async_copy(src, dst, sems.at[k]) for k, (src, dst) in enumerate(pairs)]
    for copy in copies:
        copy.start()
    return copies


def gather_kernel(
    rows_hbm, count_hbm, owner_hbm, hub_row_hbm, features_hbm,
    bundle_ref,
    rows_ref, count_ref, owner_ref, hub_row_ref, features_ref, wide_ref, hubs_ref, sems,
):
    own = lax.axis_index("dom")
    partitions = bundle_ref.shape[0]
    slots = rows_ref.shape[0]
    copies = fetch(
        [
            (features_hbm, features_ref), (rows_hbm, rows_ref), (count_hbm, count_ref),
            (owner_hbm, owner_ref), (hub_row_hbm, hub_row_ref),
        ],
        sems,
    )
    hubs_ref[...] = jnp.zeros_like(hubs_ref)
    for copy in copies:
        copy.wait()
    wide_ref[...] = features_ref[...].astype(F32)

    def hub(index, slot):
        hubs_ref[pl.ds(slots + slot, 1), :] = wide_ref[pl.ds(hub_row_ref[index], 1), :]
        return slot + (owner_ref[index] == own).astype(jnp.int32)

    repeat(owner_ref.shape[0], hub, jnp.int32(0))

    def peer(q, carry):
        bundle_ref[q] = hubs_ref[...]
        for slot in range(slots):
            row = wide_ref[pl.ds(rows_ref[slot, q], 1), :]
            bundle_ref[q, slot : slot + 1, :] = jnp.where(slot < count_ref[q], row, 0.0)
        return carry

    repeat(partitions, peer, 0)


def pack_tile(tile, dst, src):
    return tile + (dst << 8) + (src << 16)


def pad_list(list_ref, used, dst, src, group):
    spare = pack_tile(list_ref[0] & 255, dst, src)
    for k in range(group):
        list_ref[used + k] = spare


class Tiles:
    def __init__(self, list_ref, source, held, sems, columns=None):
        self.list_ref, self.source, self.held, self.sems = list_ref, source, held, sems
        self.columns = held.shape[2] if columns is None else columns

    def copy(self, tile):
        span = slice(0, self.columns)
        return pltpu.make_async_copy(
            self.source.at[tile, :, span], self.held.at[tile, :, span], self.sems.at[tile]
        )

    def start(self, total):
        def one(position, carry):
            self.copy(self.list_ref[position] & 255).start()
            return carry

        lax.fori_loop(0, total, one, 0)

    def each(self, total, size, body):
        def group(step, carry):
            codes = [self.list_ref[step * size + k] for k in range(size)]
            for k in range(size):

                @pl.when(step * size + k < total)
                def _(k=k):
                    self.copy(codes[k] & 255).wait()

            for code in codes:
                body(code & 255, (code >> 8) & 255, code >> 16)
            return carry

        lax.fori_loop(0, (total + size - 1) // size, group, 0)


def own_kernel(
    dst_hbm, src_hbm, count_hbm, features_hbm, w_self_hbm, w_neigh_hbm, bias_hbm, adjacency_hbm,
    total_hbm, far_hbm,
    dst_ref, src_ref, count_ref, features_ref, w_self_ref, w_neigh_ref, bias_ref,
    adjacency_ref, blocks_ref, total_ref, sums_ref, far_ref, list_ref, far_list_ref, sems, tile_sems, out_sems,
):
    tile_rows = adjacency_ref.shape[1]
    dst_blocks = total_ref.shape[0] - 1
    far_blocks, columns = sums_ref.shape[1], sums_ref.shape[3]
    copies = fetch(
        [
            (src_hbm, src_ref), (dst_hbm, dst_ref), (count_hbm, count_ref), (w_neigh_hbm, w_neigh_ref),
            (features_hbm, features_ref), (w_self_hbm, w_self_ref), (bias_hbm, bias_ref),
        ],
        sems,
    )
    sums_ref[...] = jnp.zeros_like(sums_ref)
    for copy in copies[:3]:
        copy.wait()
    far = Tiles(far_list_ref, adjacency_hbm, adjacency_ref, tile_sems, columns)
    near = Tiles(list_ref, adjacency_hbm, adjacency_ref, tile_sems)

    def split(tile, used):
        near_used, far_used = used
        code = pack_tile(tile, dst_ref[tile], src_ref[tile])
        list_ref[near_used] = code
        far_list_ref[far_used] = code
        is_near = (code < (dst_blocks << 16)).astype(jnp.int32)

        @pl.when(is_near == 0)
        def _():
            far.copy(tile).start()

        return near_used + is_near, far_used + 1 - is_near

    near_used, far_used = lax.fori_loop(0, count_ref[0], split, (jnp.int32(0), jnp.int32(0)))
    near.start(near_used)
    pad_list(list_ref, near_used, dst_blocks, dst_blocks, GROUP_TILES)
    pad_list(far_list_ref, far_used, dst_blocks, dst_blocks, FAR_GROUP)
    for copy in copies[3:]:
        copy.wait()
    features = features_ref[...]
    projected = dot(features, w_neigh_ref[...]).astype(BF16)
    for block in range(dst_blocks):
        blocks_ref[block] = projected[block * tile_rows : (block + 1) * tile_rows]
    blocks_ref[dst_blocks] = jnp.zeros(blocks_ref.shape[1:], BF16)
    base = dot(features, w_self_ref[...]) + bias_ref[...]
    for block in range(dst_blocks):
        total_ref[block] = base[block * tile_rows : (block + 1) * tile_rows]
    total_ref[dst_blocks] = jnp.zeros(total_ref.shape[1:], F32)

    def add_far(tile, dst, src):
        sums_ref[dst, src - dst_blocks] += adjacency_ref[tile, :, :columns].astype(F32)

    far.each(far_used, FAR_GROUP, add_far)
    for dst in range(dst_blocks):
        for block in range(far_blocks):
            far_ref[dst, :, block * columns : (block + 1) * columns] = sums_ref[dst, block].astype(BF16)
    far_out = pltpu.make_async_copy(far_ref, far_hbm.at[0:dst_blocks], out_sems.at[0])
    far_out.start()

    def forward(tile, dst, src):
        total_ref[dst] += dot(adjacency_ref[tile], blocks_ref[src])

    near.each(near_used, GROUP_TILES, forward)
    total_out = pltpu.make_async_copy(total_ref.at[0:dst_blocks], total_hbm.at[0:dst_blocks], out_sems.at[1])
    total_out.start()
    far_out.wait()
    total_out.wait()


def rest_kernel(
    dst_hbm, src_hbm, count_hbm, owner_hbm,
    arrived_ref, total_hbm, far_hbm, features_ref, w_self_ref, w_neigh_ref, cotangent_ref, adjacency_hbm,
    output_hbm, partial_ref, message_ref, keep_ref,
    halo_ref, hubs_ref, output_ref, total_ref, far_ref, rows_ref, low_rows_ref, grad_t_ref, source_t_ref,
    back_ref, adjacency_ref, list_ref, counter_ref, dst_ref, src_ref, count_ref, owner_ref, tile_sems, sems, scalar_sems,
    *, partitions, slots, columns,
):
    me = lax.axis_index("dom")
    tile_rows = adjacency_ref.shape[1]
    dst_blocks = total_ref.shape[0]
    halo_blocks = -(-partitions * slots // tile_rows)
    hub_base = halo_blocks * columns
    scalars = fetch(
        [(src_hbm, src_ref), (dst_hbm, dst_ref), (count_hbm, count_ref), (owner_hbm, owner_ref)], scalar_sems
    )
    total_in = pltpu.make_async_copy(total_hbm.at[0:dst_blocks], total_ref, sems.at[0])
    total_in.start()
    far_in = pltpu.make_async_copy(far_hbm.at[0:dst_blocks], far_ref, sems.at[1])
    far_in.start()
    rows_ref[...] = jnp.zeros_like(rows_ref)
    source_t_ref[...] = jnp.zeros_like(source_t_ref)
    grad_t_ref[dst_blocks] = jnp.zeros(grad_t_ref.shape[1:], BF16)
    for copy in scalars:
        copy.wait()
    near = Tiles(list_ref, adjacency_hbm, adjacency_ref, tile_sems)

    def find_near(tile, used):
        code = pack_tile(tile, dst_ref[tile], src_ref[tile])
        list_ref[used] = code
        is_near = code < (dst_blocks << 16)

        @pl.when(is_near)
        def _():
            near.copy(tile).start()

        return used + is_near.astype(jnp.int32)

    used = lax.fori_loop(0, count_ref[0], find_near, jnp.int32(0))
    pad_list(list_ref, used, dst_blocks, dst_blocks, GROUP_TILES)

    def halo_in(q, carry):
        rows_ref[pl.ds(q * slots, slots), :] = arrived_ref[q, 0:slots, :]
        return carry

    repeat(partitions, halo_in, 0)

    def hub_in(hub, owner, slot):
        rows_ref[pl.ds(hub_base + hub, 1), :] = arrived_ref[owner, pl.ds(slots + slot, 1), :]

    hub_slots(owner_ref, counter_ref, partitions, hub_in)
    low_rows = rows_ref[...].astype(BF16)
    low_rows_ref[...] = low_rows
    far_projected = dot(low_rows, w_neigh_ref[...]).astype(BF16)
    total_in.wait()
    far_in.wait()

    root = 0.7978845608028654
    bias_sum = jnp.zeros((1, output_ref.shape[1]), F32)
    w_self_t = jnp.zeros((output_ref.shape[1], features_ref.shape[1]), F32)
    far_t = jnp.zeros((output_ref.shape[1], far_ref.shape[2]), F32)
    for block in range(dst_blocks):
        span = slice(block * tile_rows, (block + 1) * tile_rows)
        v = total_ref[block] + dot(far_ref[block], far_projected)
        square = v * v
        gate = jnp.tanh(root * (v + 0.044715 * (v * square)))
        half = 0.5 * (1.0 + gate)
        output_ref[span, :] = (v * half).astype(BF16)
        slope = half + (0.5 * root) * v * (1.0 - gate * gate) * (1.0 + (3 * 0.044715) * square)
        grad = cotangent_ref[span, :].astype(F32) * slope
        bias_sum += jnp.sum(grad, axis=0, keepdims=True)
        low_t = jnp.transpose(grad.astype(BF16))
        grad_t_ref[block] = low_t
        partial_ref[span, :] = dot_nt(grad.astype(BF16), w_self_ref[...])
        w_self_t += dot(low_t, features_ref[span, :])
        far_t += dot(low_t, far_ref[block])
    output_out = pltpu.make_async_copy(output_ref, output_hbm, sems.at[2])
    output_out.start()

    def backward(tile, dst, src):
        source_t_ref[src] += dot(grad_t_ref[dst], adjacency_ref[tile])

    near.each(used, GROUP_TILES, backward)

    back_ref[...] = dot_nt(jnp.transpose(far_t.astype(BF16)), w_neigh_ref[...])
    w_neigh_t = dot(far_t.astype(BF16), low_rows_ref[...])
    for block in range(dst_blocks):
        span = slice(block * tile_rows, (block + 1) * tile_rows)
        source_t = source_t_ref[block].astype(BF16)
        w_neigh_t += dot(source_t, features_ref[span, :])
        partial_ref[span, :] += dot_nt(jnp.transpose(source_t), w_neigh_ref[...])

    def halo_out(q, carry):
        halo_ref[pl.ds((q ^ me) * slots, slots), :] = back_ref[pl.ds(q * slots, slots), :]
        return carry

    repeat(partitions, halo_out, 0)
    hubs_ref[...] = jnp.zeros_like(hubs_ref)

    def hub_out(hub, owner, slot):
        hubs_ref[pl.ds((owner ^ me) * HUB_MOST + slot, 1), :] = back_ref[pl.ds(hub_base + hub, 1), :]

    hub_slots(owner_ref, counter_ref, partitions, hub_out)
    plan = Exchange(partitions, slots, 0)
    message_ref[0 : plan.weights, :] = jnp.concatenate([w_self_t, w_neigh_t], axis=0).astype(BF16)
    plan.write(message_ref, keep_ref, halo_ref[...], hubs_ref[...], bias_sum)
    output_out.wait()


class Exchange:
    weights = 256

    def __init__(self, partitions, slots, step):
        self.groups = 1 << step
        self.half = partitions >> (step + 1)
        self.slots = slots
        self.halo = self.groups * self.half * slots
        self.hub = self.half * HUB_MOST
        self.keep = self.halo + self.hub
        self.rows = self.weights + -(-(self.keep + 2) // 16) * 16

    def halves(self, rows, width):
        lower, upper = [], []
        span = self.half * width
        for group in range(rows.shape[0] // (2 * span)):
            base = 2 * group * span
            lower.append(rows[base : base + span])
            upper.append(rows[base + span : base + 2 * span])
        return lower, upper

    def write(self, message_ref, keep_ref, halo, hubs, bias):
        halo_keep, halo_send = self.halves(halo, self.slots)
        hub_keep, hub_send = self.halves(hubs, HUB_MOST)
        high = bias.astype(BF16).astype(F32)
        spare = self.rows - self.weights - self.keep - 2
        parts = halo_send + hub_send + [high, bias - high]
        if spare:
            parts.append(jnp.zeros((spare, bias.shape[1]), F32))
        sent = jnp.concatenate(parts, axis=0).astype(BF16)
        message_ref[self.weights : self.rows, :] = sent
        keep_ref[...] = jnp.concatenate(halo_keep + hub_keep, axis=0)
        return sent

    def tail(self, ref):
        return ref[self.weights : self.rows, :].astype(F32)

    def bias(self, own, other):
        k = self.keep
        return (own[k : k + 1] + own[k + 1 : k + 2]) + (other[k : k + 1] + other[k + 1 : k + 2])

    def merged(self, keep, other):
        halo = jnp.concatenate([keep[: self.halo], other[: self.halo]], axis=0)
        return halo, keep[self.halo :] + other[self.halo : self.keep]

    def weight_sum(self, sent_ref, got_ref):
        rows = slice(0, self.weights)
        return sent_ref[rows, :].astype(F32) + got_ref[rows, :].astype(F32)


def step_kernel(sent_ref, got_ref, keep_ref, message_ref, next_keep_ref, *tail_refs, now, then):
    message_ref[0 : now.weights, :] = now.weight_sum(sent_ref, got_ref).astype(BF16)
    other = now.tail(got_ref)
    halo, hubs = now.merged(keep_ref[...], other)
    sent = then.write(message_ref, next_keep_ref, halo, hubs, now.bias(now.tail(sent_ref), other))
    for tail_ref in tail_refs:
        tail_ref[...] = sent


def prepare_kernel(
    rows_ref, count_ref, owner_ref, hub_row_ref, partial_ref, other_partial_ref, total_ref, target_ref
):
    me = lax.axis_index("dom")
    slots, partitions = rows_ref.shape
    nodes = partial_ref.shape[0]
    steps = partitions.bit_length() - 1
    total_ref[...] = partial_ref[...] + other_partial_ref[...]
    for group in range(partitions):
        origin = me ^ sum(((group >> k) & 1) << (steps - 1 - k) for k in range(steps))
        for slot in range(slots):
            sent = slot < count_ref[origin]
            target_ref[group * slots + slot] = jnp.where(sent, rows_ref[slot, origin], nodes)
    base = partitions * slots
    for slot in range(HUB_MOST):
        target_ref[base + slot] = nodes

    def hub(index, slot):
        mine = (owner_ref[index] == me).astype(jnp.int32)
        target_ref[base + slot] = jnp.where(mine == 1, hub_row_ref[index], nodes)
        return slot + mine

    repeat(owner_ref.shape[0], hub, jnp.int32(0))


def final_kernel(
    target_hbm, sent_ref, got_ref, cross_ref, keep_ref, other_keep_ref, total_in_ref,
    w_self_ref, w_neigh_ref, bias_ref, low_ref, total_ref, target_ref, sem, *, now,
):
    nodes = total_in_ref.shape[0]
    target_in = pltpu.make_async_copy(target_hbm, target_ref, sem)
    target_in.start()
    total_ref[0:nodes, :] = total_in_ref[...]
    got = now.tail(got_ref)
    keep = keep_ref[...] + other_keep_ref[...]
    halo, hubs = now.merged(keep, got + cross_ref[...].astype(F32))
    returned = jnp.concatenate([halo, hubs], axis=0)
    target_in.wait()
    for place in range(returned.shape[0]):
        row = pl.ds(target_ref[place], 1)
        total_ref[row, :] += returned[place : place + 1, :]
    low_ref[...] = total_ref[0:nodes, :].astype(BF16)
    weights = now.weight_sum(sent_ref, got_ref)
    split = now.weights // 2
    w_self_ref[...] = jnp.transpose(weights[:split])
    w_neigh_ref[...] = jnp.transpose(weights[split:])
    bias_ref[...] = now.bias(now.tail(sent_ref), got)


SMEM = pl.BlockSpec(memory_space=pltpu.SMEM)
VMEM = pl.BlockSpec(memory_space=pltpu.VMEM)
HBM = pl.BlockSpec(memory_space=pltpu.HBM)


def call(kernel, name, ins, outs, scratch, args, grant, flops=0, size=0, out_specs=None):
    return pl.pallas_call(
        kernel,
        out_shape=outs,
        in_specs=ins,
        out_specs=jax.tree.map(lambda _: VMEM, outs) if out_specs is None else out_specs,
        scratch_shapes=scratch,
        compiler_params=pltpu.CompilerParams(vmem_limit_bytes=grant * 1024 * 1024),
        cost_estimate=pl.CostEstimate(flops=flops, bytes_accessed=size, transcendentals=0),
        name=name,
    )(*args)


def local(
    features, w_self, w_neigh, bias, cotangent, adjacency, tile_dst, tile_src, tile_count,
    send_rows, send_count, hub_owner, hub_row,
):
    nodes, inputs = features.shape
    limit, tile_rows, _ = adjacency.shape
    hidden = w_neigh.shape[1]
    partitions = lax.axis_size("dom")
    slots = send_rows.shape[2]
    hubs = hub_row.shape[0]
    dst_blocks = nodes // tile_rows
    far_blocks = -(-partitions * slots // tile_rows) - (-hubs // tile_rows)
    columns = min(tile_rows, -(-max(partitions * slots, hubs) // 128) * 128)
    rows = jnp.transpose(send_rows[0])
    counts = send_count.reshape(partitions)
    owner = hub_owner.reshape(hubs)
    struct = jax.ShapeDtypeStruct
    lists = pltpu.SMEM((limit + GROUP_TILES,), jnp.int32)

    bundle = call(
        gather_kernel, "gather", [HBM] * 5,
        struct((partitions, PEER_ROWS, inputs), F32),
        [
            pltpu.SMEM((slots, partitions), jnp.int32),
            pltpu.SMEM((partitions,), jnp.int32),
            pltpu.SMEM((hubs,), jnp.int32),
            pltpu.SMEM((hubs,), jnp.int32),
            pltpu.VMEM((nodes, inputs), BF16),
            pltpu.VMEM((nodes, inputs), F32),
            pltpu.VMEM((PEER_ROWS, inputs), F32),
            pltpu.SemaphoreType.DMA((5,)),
        ],
        (rows, counts, owner, hub_row, features), 60,
    )
    arrived = lax.all_to_all(bundle, "dom", split_axis=0, concat_axis=0, tiled=True)
    total, far = call(
        own_kernel, "own_tiles", [HBM] * 8,
        (
            struct((limit, tile_rows, hidden), F32),
            struct((limit, tile_rows, far_blocks * columns), BF16),
        ),
        [
            pltpu.SMEM((limit,), jnp.int32),
            pltpu.SMEM((limit,), jnp.int32),
            pltpu.SMEM((1,), jnp.int32),
            pltpu.VMEM((nodes, inputs), BF16),
            pltpu.VMEM((inputs, hidden), BF16),
            pltpu.VMEM((inputs, hidden), BF16),
            pltpu.VMEM((1, hidden), F32),
            pltpu.VMEM(adjacency.shape, BF16),
            pltpu.VMEM((dst_blocks + 1, tile_rows, hidden), BF16),
            pltpu.VMEM((dst_blocks + 1, tile_rows, hidden), F32),
            pltpu.VMEM((dst_blocks + 1, far_blocks, tile_rows, columns), F32),
            pltpu.VMEM((dst_blocks, tile_rows, far_blocks * columns), BF16),
            lists,
            lists,
            pltpu.SemaphoreType.DMA((7,)),
            pltpu.SemaphoreType.DMA((limit,)),
            pltpu.SemaphoreType.DMA((2,)),
        ],
        (tile_dst, tile_src, tile_count, features, w_self, w_neigh, bias.reshape(1, hidden), adjacency),
        54, flops=2 * limit * tile_rows * tile_rows * hidden, size=adjacency.size * 2, out_specs=(HBM, HBM),
    )
    plans = [Exchange(partitions, slots, step) for step in range(partitions.bit_length() - 1)]
    output, partial, message, keep = call(
        functools.partial(rest_kernel, partitions=partitions, slots=slots, columns=columns), "rest",
        [HBM] * 4 + [VMEM, HBM, HBM] + [VMEM] * 4 + [HBM],
        (
            struct((nodes, hidden), BF16),
            struct((nodes, inputs), F32),
            struct((plans[0].rows, inputs), BF16),
            struct((plans[0].keep, inputs), F32),
        ),
        [
            pltpu.VMEM((partitions * slots, inputs), F32),
            pltpu.VMEM((partitions * HUB_MOST, inputs), F32),
            pltpu.VMEM((nodes, hidden), BF16),
            pltpu.VMEM((dst_blocks, tile_rows, hidden), F32),
            pltpu.VMEM((dst_blocks, tile_rows, far_blocks * columns), BF16),
            pltpu.VMEM((far_blocks * columns, inputs), F32),
            pltpu.VMEM((far_blocks * columns, inputs), BF16),
            pltpu.VMEM((dst_blocks + 1, hidden, tile_rows), BF16),
            pltpu.VMEM((dst_blocks + 1, hidden, tile_rows), F32),
            pltpu.VMEM((far_blocks * columns, inputs), F32),
            pltpu.VMEM(adjacency.shape, BF16),
            lists,
            pltpu.SMEM((partitions,), jnp.int32),
            pltpu.SMEM((limit,), jnp.int32),
            pltpu.SMEM((limit,), jnp.int32),
            pltpu.SMEM((1,), jnp.int32),
            pltpu.SMEM((hubs,), jnp.int32),
            pltpu.SemaphoreType.DMA((limit,)),
            pltpu.SemaphoreType.DMA((3,)),
            pltpu.SemaphoreType.DMA((4,)),
        ],
        (
            tile_dst, tile_src, tile_count, owner,
            arrived, total, far, features, w_self, w_neigh, cotangent, adjacency,
        ),
        50, out_specs=(HBM, VMEM, VMEM, VMEM),
    )
    swap = [(0, 1), (1, 0)]
    tail = None
    for now, then in zip(plans, plans[1:]):
        got = lax.ppermute(message, "dom", [(q, q ^ now.half) for q in range(partitions)])
        if now is plans[0]:
            got, late_partial = lax.optimization_barrier((got, partial))
        outs = [struct((then.rows, inputs), BF16), struct((then.keep, inputs), F32)]
        if then is plans[-1]:
            outs.append(struct((then.rows - then.weights, inputs), BF16))
        message, keep, *tail = call(
            functools.partial(step_kernel, now=now, then=then), "step", [VMEM] * 3,
            tuple(outs), [], (message, got, keep), 16,
        )
    now = plans[-1]
    got = lax.ppermute(message, "dom", [(q, q ^ 1) for q in range(partitions)])
    cross = lax.ppermute(tail[0], ("dom", "feat"), [(k, k ^ 3) for k in range(2 * partitions)])
    other_keep = lax.ppermute(keep, "feat", swap)
    other_partial = lax.ppermute(late_partial, "feat", swap)
    summed, target = call(
        prepare_kernel, "prepare", [SMEM] * 4 + [VMEM] * 2,
        (struct((nodes, inputs), F32), struct((partitions * slots + HUB_MOST + 1,), jnp.int32)),
        [], (rows, counts, owner, hub_row, partial, other_partial), 16,
        flops=10**6, size=4 * 10**6, out_specs=(VMEM, SMEM),
    )
    grad_w_self, grad_w_neigh, grad_bias, grad_features = call(
        functools.partial(final_kernel, now=now), "final", [HBM] + [VMEM] * 6,
        (
            struct((inputs, hidden), F32), struct((inputs, hidden), F32), struct((1, hidden), F32),
            struct((nodes, inputs), BF16),
        ),
        [
            pltpu.VMEM((nodes + 8, inputs), F32),
            pltpu.SMEM((partitions * slots + HUB_MOST + 1,), jnp.int32),
            pltpu.SemaphoreType.DMA,
        ],
        (target, message, got, cross, keep, other_keep, summed), 32,
    )
    return (output, grad_features, grad_w_self, grad_w_neigh, grad_bias.reshape(hidden))


def solution(mesh):
    return jax.shard_map(
        local,
        mesh=mesh,
        in_specs=(
            P(("group", "dom"), None),
            P(None, "feat"),
            P(None, "feat"),
            P("feat"),
            P(("group", "dom"), "feat"),
            P(("group", "dom"), None, None),
            P(("group", "dom")),
            P(("group", "dom")),
            P(("group", "dom")),
            P(("group", "dom"), None, None),
            P(("group", "dom"), None),
            P("group", None),
            P("group"),
        ),
        out_specs=(
            P(("group", "dom"), "feat"),
            P(("group", "dom"), None),
            P("group", "feat"),
            P("group", "feat"),
            P(("group", "feat")),
        ),
        check_vma=False,
    )
```

```python
import functools

import jax
import jax.numpy as jnp
from jax import lax
from jax.experimental import pallas as pl
from jax.experimental.pallas import tpu as pltpu
from jax.sharding import PartitionSpec as P

HUB_MOST = 4
PEER_ROWS = 8
GROUP_TILES = 8
FAR_GROUP = 4
F32 = jnp.float32
BF16 = jnp.bfloat16
NT = (((1,), (1,)), ((), ()))


def dot(a, b):
    return jnp.dot(a, b, preferred_element_type=F32)


def dot_nt(a, b):
    return lax.dot_general(a, b, NT, preferred_element_type=F32)


def repeat(count, body, init):
    return lax.fori_loop(0, count, body, init, unroll=True)


def hub_slots(owner_ref, counter_ref, partitions, body):
    def clear(q, carry):
        counter_ref[q] = 0
        return carry

    def visit(hub, carry):
        owner = owner_ref[hub]
        slot = counter_ref[owner]
        counter_ref[owner] = slot + 1
        body(hub, owner, slot)
        return carry

    repeat(partitions, clear, 0)
    repeat(owner_ref.shape[0], visit, 0)


def fetch(pairs, sems):
    copies = [pltpu.make_async_copy(src, dst, sems.at[k]) for k, (src, dst) in enumerate(pairs)]
    for copy in copies:
        copy.start()
    return copies


def gather_kernel(
    rows_hbm, count_hbm, owner_hbm, hub_row_hbm, features_hbm,
    bundle_ref,
    rows_ref, count_ref, owner_ref, hub_row_ref, features_ref, wide_ref, hubs_ref, sems,
):
    own = lax.axis_index("dom")
    partitions = bundle_ref.shape[0]
    slots = rows_ref.shape[0]
    copies = fetch(
        [
            (features_hbm, features_ref), (rows_hbm, rows_ref), (count_hbm, count_ref),
            (owner_hbm, owner_ref), (hub_row_hbm, hub_row_ref),
        ],
        sems,
    )
    hubs_ref[...] = jnp.zeros_like(hubs_ref)
    for copy in copies:
        copy.wait()
    wide_ref[...] = features_ref[...].astype(F32)

    def hub(index, slot):
        hubs_ref[pl.ds(slots + slot, 1), :] = wide_ref[pl.ds(hub_row_ref[index], 1), :]
        return slot + (owner_ref[index] == own).astype(jnp.int32)

    repeat(owner_ref.shape[0], hub, jnp.int32(0))

    def peer(q, carry):
        bundle_ref[q] = hubs_ref[...]
        for slot in range(slots):
            row = wide_ref[pl.ds(rows_ref[slot, q], 1), :]
            bundle_ref[q, slot : slot + 1, :] = jnp.where(slot < count_ref[q], row, 0.0)
        return carry

    repeat(partitions, peer, 0)


def pack_tile(tile, dst, src):
    return tile + (dst << 8) + (src << 16)


def pad_list(list_ref, used, dst, src, group):
    spare = pack_tile(list_ref[0] & 255, dst, src)
    for k in range(group):
        list_ref[used + k] = spare


class Tiles:
    def __init__(self, list_ref, source, held, sems, columns=None):
        self.list_ref, self.source, self.held, self.sems = list_ref, source, held, sems
        self.columns = held.shape[2] if columns is None else columns

    def copy(self, tile):
        span = slice(0, self.columns)
        return pltpu.make_async_copy(
            self.source.at[tile, :, span], self.held.at[tile, :, span], self.sems.at[tile]
        )

    def start(self, total):
        def one(position, carry):
            self.copy(self.list_ref[position] & 255).start()
            return carry

        lax.fori_loop(0, total, one, 0)

    def each(self, total, size, body):
        def group(step, carry):
            codes = [self.list_ref[step * size + k] for k in range(size)]
            for k in range(size):

                @pl.when(step * size + k < total)
                def _(k=k):
                    self.copy(codes[k] & 255).wait()

            for code in codes:
                body(code & 255, (code >> 8) & 255, code >> 16)
            return carry

        lax.fori_loop(0, (total + size - 1) // size, group, 0)


def own_kernel(
    dst_hbm, src_hbm, count_hbm, features_hbm, w_self_hbm, w_neigh_hbm, bias_hbm, adjacency_hbm,
    total_hbm, far_hbm,
    dst_ref, src_ref, count_ref, features_ref, w_self_ref, w_neigh_ref, bias_ref,
    adjacency_ref, blocks_ref, total_ref, sums_ref, far_ref, list_ref, far_list_ref, sems, tile_sems, out_sems,
):
    tile_rows = adjacency_ref.shape[1]
    dst_blocks = total_ref.shape[0] - 1
    far_blocks, columns = sums_ref.shape[1], sums_ref.shape[3]
    copies = fetch(
        [
            (src_hbm, src_ref), (dst_hbm, dst_ref), (count_hbm, count_ref), (w_neigh_hbm, w_neigh_ref),
            (features_hbm, features_ref), (w_self_hbm, w_self_ref), (bias_hbm, bias_ref),
        ],
        sems,
    )
    sums_ref[...] = jnp.zeros_like(sums_ref)
    for copy in copies[:3]:
        copy.wait()
    far = Tiles(far_list_ref, adjacency_hbm, adjacency_ref, tile_sems, columns)
    near = Tiles(list_ref, adjacency_hbm, adjacency_ref, tile_sems)

    def split(tile, used):
        near_used, far_used = used
        code = pack_tile(tile, dst_ref[tile], src_ref[tile])
        list_ref[near_used] = code
        far_list_ref[far_used] = code
        is_near = (code < (dst_blocks << 16)).astype(jnp.int32)

        @pl.when(is_near == 0)
        def _():
            far.copy(tile).start()

        @pl.when(is_near == 1)
        def _():
            near.copy(tile).start()

        return near_used + is_near, far_used + 1 - is_near

    near_used, far_used = lax.fori_loop(0, count_ref[0], split, (jnp.int32(0), jnp.int32(0)))
    pad_list(list_ref, near_used, dst_blocks, dst_blocks, GROUP_TILES)
    pad_list(far_list_ref, far_used, dst_blocks, dst_blocks, FAR_GROUP)
    for copy in copies[3:]:
        copy.wait()
    features = features_ref[...]
    projected = dot(features, w_neigh_ref[...]).astype(BF16)
    for block in range(dst_blocks):
        blocks_ref[block] = projected[block * tile_rows : (block + 1) * tile_rows]
    blocks_ref[dst_blocks] = jnp.zeros(blocks_ref.shape[1:], BF16)
    base = dot(features, w_self_ref[...]) + bias_ref[...]
    for block in range(dst_blocks):
        total_ref[block] = base[block * tile_rows : (block + 1) * tile_rows]
    total_ref[dst_blocks] = jnp.zeros(total_ref.shape[1:], F32)

    def forward(tile, dst, src):
        total_ref[dst] += dot(adjacency_ref[tile], blocks_ref[src])

    near.each(near_used, GROUP_TILES, forward)
    total_out = pltpu.make_async_copy(total_ref.at[0:dst_blocks], total_hbm.at[0:dst_blocks], out_sems.at[1])
    total_out.start()

    def add_far(tile, dst, src):
        sums_ref[dst, src - dst_blocks] += adjacency_ref[tile, :, :columns].astype(F32)

    far.each(far_used, FAR_GROUP, add_far)
    for dst in range(dst_blocks):
        for block in range(far_blocks):
            far_ref[dst, :, block * columns : (block + 1) * columns] = sums_ref[dst, block].astype(BF16)
    far_out = pltpu.make_async_copy(far_ref, far_hbm.at[0:dst_blocks], out_sems.at[0])
    far_out.start()
    far_out.wait()
    total_out.wait()


def rest_kernel(
    dst_hbm, src_hbm, count_hbm, owner_hbm,
    arrived_ref, total_hbm, far_hbm, features_ref, w_self_ref, w_neigh_ref, cotangent_ref, adjacency_hbm,
    output_hbm, partial_ref, message_ref, keep_ref,
    halo_ref, hubs_ref, output_ref, total_ref, far_ref, rows_ref, low_rows_ref, grad_t_ref, source_t_ref,
    back_ref, adjacency_ref, list_ref, counter_ref, dst_ref, src_ref, count_ref, owner_ref, tile_sems, sems, scalar_sems,
    *, partitions, slots, columns,
):
    me = lax.axis_index("dom")
    tile_rows = adjacency_ref.shape[1]
    dst_blocks = total_ref.shape[0]
    halo_blocks = -(-partitions * slots // tile_rows)
    hub_base = halo_blocks * columns
    scalars = fetch(
        [(src_hbm, src_ref), (dst_hbm, dst_ref), (count_hbm, count_ref), (owner_hbm, owner_ref)], scalar_sems
    )
    total_in = pltpu.make_async_copy(total_hbm.at[0:dst_blocks], total_ref, sems.at[0])
    total_in.start()
    far_in = pltpu.make_async_copy(far_hbm.at[0:dst_blocks], far_ref, sems.at[1])
    far_in.start()
    rows_ref[...] = jnp.zeros_like(rows_ref)
    source_t_ref[...] = jnp.zeros_like(source_t_ref)
    grad_t_ref[dst_blocks] = jnp.zeros(grad_t_ref.shape[1:], BF16)
    for copy in scalars:
        copy.wait()
    near = Tiles(list_ref, adjacency_hbm, adjacency_ref, tile_sems)

    def find_near(tile, used):
        code = pack_tile(tile, dst_ref[tile], src_ref[tile])
        list_ref[used] = code
        is_near = code < (dst_blocks << 16)

        @pl.when(is_near)
        def _():
            near.copy(tile).start()

        return used + is_near.astype(jnp.int32)

    used = lax.fori_loop(0, count_ref[0], find_near, jnp.int32(0))
    pad_list(list_ref, used, dst_blocks, dst_blocks, GROUP_TILES)

    def halo_in(q, carry):
        rows_ref[pl.ds(q * slots, slots), :] = arrived_ref[q, 0:slots, :]
        return carry

    repeat(partitions, halo_in, 0)

    def hub_in(hub, owner, slot):
        rows_ref[pl.ds(hub_base + hub, 1), :] = arrived_ref[owner, pl.ds(slots + slot, 1), :]

    hub_slots(owner_ref, counter_ref, partitions, hub_in)
    low_rows = rows_ref[...].astype(BF16)
    low_rows_ref[...] = low_rows
    far_projected = dot(low_rows, w_neigh_ref[...]).astype(BF16)
    total_in.wait()
    far_in.wait()

    root = 0.7978845608028654
    bias_sum = jnp.zeros((1, output_ref.shape[1]), F32)
    w_self_t = jnp.zeros((output_ref.shape[1], features_ref.shape[1]), F32)
    far_t = jnp.zeros((output_ref.shape[1], far_ref.shape[2]), F32)
    for block in range(dst_blocks):
        span = slice(block * tile_rows, (block + 1) * tile_rows)
        v = total_ref[block] + dot(far_ref[block], far_projected)
        square = v * v
        gate = jnp.tanh(root * (v + 0.044715 * (v * square)))
        half = 0.5 * (1.0 + gate)
        output_ref[span, :] = (v * half).astype(BF16)
        slope = half + (0.5 * root) * v * (1.0 - gate * gate) * (1.0 + (3 * 0.044715) * square)
        grad = cotangent_ref[span, :].astype(F32) * slope
        bias_sum += jnp.sum(grad, axis=0, keepdims=True)
        low_t = jnp.transpose(grad.astype(BF16))
        grad_t_ref[block] = low_t
        partial_ref[span, :] = dot_nt(grad.astype(BF16), w_self_ref[...])
        w_self_t += dot(low_t, features_ref[span, :])
        far_t += dot(low_t, far_ref[block])
    output_out = pltpu.make_async_copy(output_ref, output_hbm, sems.at[2])
    output_out.start()

    def backward(tile, dst, src):
        source_t_ref[src] += dot(grad_t_ref[dst], adjacency_ref[tile])

    near.each(used, GROUP_TILES, backward)

    back_ref[...] = dot_nt(jnp.transpose(far_t.astype(BF16)), w_neigh_ref[...])
    w_neigh_t = dot(far_t.astype(BF16), low_rows_ref[...])
    for block in range(dst_blocks):
        span = slice(block * tile_rows, (block + 1) * tile_rows)
        source_t = source_t_ref[block].astype(BF16)
        w_neigh_t += dot(source_t, features_ref[span, :])
        partial_ref[span, :] += dot_nt(jnp.transpose(source_t), w_neigh_ref[...])

    def halo_out(q, carry):
        halo_ref[pl.ds((q ^ me) * slots, slots), :] = back_ref[pl.ds(q * slots, slots), :]
        return carry

    repeat(partitions, halo_out, 0)
    hubs_ref[...] = jnp.zeros_like(hubs_ref)

    def hub_out(hub, owner, slot):
        hubs_ref[pl.ds((owner ^ me) * HUB_MOST + slot, 1), :] = back_ref[pl.ds(hub_base + hub, 1), :]

    hub_slots(owner_ref, counter_ref, partitions, hub_out)
    plan = Exchange(partitions, slots, 0)
    message_ref[0 : plan.weights, :] = jnp.concatenate([w_self_t, w_neigh_t], axis=0).astype(BF16)
    plan.write(message_ref, keep_ref, halo_ref[...], hubs_ref[...], bias_sum)
    output_out.wait()


class Exchange:
    weights = 256

    def __init__(self, partitions, slots, step):
        self.groups = 1 << step
        self.half = partitions >> (step + 1)
        self.slots = slots
        self.halo = self.groups * self.half * slots
        self.hub = self.half * HUB_MOST
        self.keep = self.halo + self.hub
        self.rows = self.weights + -(-(self.keep + 2) // 16) * 16

    def halves(self, rows, width):
        lower, upper = [], []
        span = self.half * width
        for group in range(rows.shape[0] // (2 * span)):
            base = 2 * group * span
            lower.append(rows[base : base + span])
            upper.append(rows[base + span : base + 2 * span])
        return lower, upper

    def write(self, message_ref, keep_ref, halo, hubs, bias):
        halo_keep, halo_send = self.halves(halo, self.slots)
        hub_keep, hub_send = self.halves(hubs, HUB_MOST)
        high = bias.astype(BF16).astype(F32)
        spare = self.rows - self.weights - self.keep - 2
        parts = halo_send + hub_send + [high, bias - high]
        if spare:
            parts.append(jnp.zeros((spare, bias.shape[1]), F32))
        sent = jnp.concatenate(parts, axis=0).astype(BF16)
        message_ref[self.weights : self.rows, :] = sent
        keep_ref[...] = jnp.concatenate(halo_keep + hub_keep, axis=0)
        return sent

    def tail(self, ref):
        return ref[self.weights : self.rows, :].astype(F32)

    def bias(self, own, other):
        k = self.keep
        return (own[k : k + 1] + own[k + 1 : k + 2]) + (other[k : k + 1] + other[k + 1 : k + 2])

    def merged(self, keep, other):
        halo = jnp.concatenate([keep[: self.halo], other[: self.halo]], axis=0)
        return halo, keep[self.halo :] + other[self.halo : self.keep]

    def weight_sum(self, sent_ref, got_ref):
        rows = slice(0, self.weights)
        return sent_ref[rows, :].astype(F32) + got_ref[rows, :].astype(F32)


def step_kernel(sent_ref, got_ref, keep_ref, message_ref, next_keep_ref, *tail_refs, now, then):
    message_ref[0 : now.weights, :] = now.weight_sum(sent_ref, got_ref).astype(BF16)
    other = now.tail(got_ref)
    halo, hubs = now.merged(keep_ref[...], other)
    sent = then.write(message_ref, next_keep_ref, halo, hubs, now.bias(now.tail(sent_ref), other))
    for tail_ref in tail_refs:
        tail_ref[...] = sent


def prepare_kernel(
    rows_ref, count_ref, owner_ref, hub_row_ref, partial_ref, other_partial_ref, total_ref, target_ref
):
    me = lax.axis_index("dom")
    slots, partitions = rows_ref.shape
    nodes = partial_ref.shape[0]
    steps = partitions.bit_length() - 1
    total_ref[...] = partial_ref[...] + other_partial_ref[...]
    for group in range(partitions):
        origin = me ^ sum(((group >> k) & 1) << (steps - 1 - k) for k in range(steps))
        for slot in range(slots):
            sent = slot < count_ref[origin]
            target_ref[group * slots + slot] = jnp.where(sent, rows_ref[slot, origin], nodes)
    base = partitions * slots
    for slot in range(HUB_MOST):
        target_ref[base + slot] = nodes

    def hub(index, slot):
        mine = (owner_ref[index] == me).astype(jnp.int32)
        target_ref[base + slot] = jnp.where(mine == 1, hub_row_ref[index], nodes)
        return slot + mine

    repeat(owner_ref.shape[0], hub, jnp.int32(0))


def final_kernel(
    target_hbm, sent_ref, got_ref, cross_ref, keep_ref, other_keep_ref, total_in_ref,
    w_self_ref, w_neigh_ref, bias_ref, low_ref, total_ref, target_ref, sem, *, now,
):
    nodes = total_in_ref.shape[0]
    target_in = pltpu.make_async_copy(target_hbm, target_ref, sem)
    target_in.start()
    total_ref[0:nodes, :] = total_in_ref[...]
    got = now.tail(got_ref)
    keep = keep_ref[...] + other_keep_ref[...]
    halo, hubs = now.merged(keep, got + cross_ref[...].astype(F32))
    returned = jnp.concatenate([halo, hubs], axis=0)
    target_in.wait()
    for place in range(returned.shape[0]):
        row = pl.ds(target_ref[place], 1)
        total_ref[row, :] += returned[place : place + 1, :]
    low_ref[...] = total_ref[0:nodes, :].astype(BF16)
    weights = now.weight_sum(sent_ref, got_ref)
    split = now.weights // 2
    w_self_ref[...] = jnp.transpose(weights[:split])
    w_neigh_ref[...] = jnp.transpose(weights[split:])
    bias_ref[...] = now.bias(now.tail(sent_ref), got)


SMEM = pl.BlockSpec(memory_space=pltpu.SMEM)
VMEM = pl.BlockSpec(memory_space=pltpu.VMEM)
HBM = pl.BlockSpec(memory_space=pltpu.HBM)


def call(kernel, name, ins, outs, scratch, args, grant, flops=0, size=0, out_specs=None):
    return pl.pallas_call(
        kernel,
        out_shape=outs,
        in_specs=ins,
        out_specs=jax.tree.map(lambda _: VMEM, outs) if out_specs is None else out_specs,
        scratch_shapes=scratch,
        compiler_params=pltpu.CompilerParams(vmem_limit_bytes=grant * 1024 * 1024),
        cost_estimate=pl.CostEstimate(flops=flops, bytes_accessed=size, transcendentals=0),
        name=name,
    )(*args)


def local(
    features, w_self, w_neigh, bias, cotangent, adjacency, tile_dst, tile_src, tile_count,
    send_rows, send_count, hub_owner, hub_row,
):
    nodes, inputs = features.shape
    limit, tile_rows, _ = adjacency.shape
    hidden = w_neigh.shape[1]
    partitions = lax.axis_size("dom")
    slots = send_rows.shape[2]
    hubs = hub_row.shape[0]
    dst_blocks = nodes // tile_rows
    far_blocks = -(-partitions * slots // tile_rows) - (-hubs // tile_rows)
    columns = min(tile_rows, -(-max(partitions * slots, hubs) // 128) * 128)
    rows = jnp.transpose(send_rows[0])
    counts = send_count.reshape(partitions)
    owner = hub_owner.reshape(hubs)
    struct = jax.ShapeDtypeStruct
    lists = pltpu.SMEM((limit + GROUP_TILES,), jnp.int32)

    bundle = call(
        gather_kernel, "gather", [HBM] * 5,
        struct((partitions, PEER_ROWS, inputs), F32),
        [
            pltpu.SMEM((slots, partitions), jnp.int32),
            pltpu.SMEM((partitions,), jnp.int32),
            pltpu.SMEM((hubs,), jnp.int32),
            pltpu.SMEM((hubs,), jnp.int32),
            pltpu.VMEM((nodes, inputs), BF16),
            pltpu.VMEM((nodes, inputs), F32),
            pltpu.VMEM((PEER_ROWS, inputs), F32),
            pltpu.SemaphoreType.DMA((5,)),
        ],
        (rows, counts, owner, hub_row, features), 60,
    )
    arrived = lax.all_to_all(bundle, "dom", split_axis=0, concat_axis=0, tiled=True)
    total, far = call(
        own_kernel, "own_tiles", [HBM] * 8,
        (
            struct((limit, tile_rows, hidden), F32),
            struct((limit, tile_rows, far_blocks * columns), BF16),
        ),
        [
            pltpu.SMEM((limit,), jnp.int32),
            pltpu.SMEM((limit,), jnp.int32),
            pltpu.SMEM((1,), jnp.int32),
            pltpu.VMEM((nodes, inputs), BF16),
            pltpu.VMEM((inputs, hidden), BF16),
            pltpu.VMEM((inputs, hidden), BF16),
            pltpu.VMEM((1, hidden), F32),
            pltpu.VMEM(adjacency.shape, BF16),
            pltpu.VMEM((dst_blocks + 1, tile_rows, hidden), BF16),
            pltpu.VMEM((dst_blocks + 1, tile_rows, hidden), F32),
            pltpu.VMEM((dst_blocks + 1, far_blocks, tile_rows, columns), F32),
            pltpu.VMEM((dst_blocks, tile_rows, far_blocks * columns), BF16),
            lists,
            lists,
            pltpu.SemaphoreType.DMA((7,)),
            pltpu.SemaphoreType.DMA((limit,)),
            pltpu.SemaphoreType.DMA((2,)),
        ],
        (tile_dst, tile_src, tile_count, features, w_self, w_neigh, bias.reshape(1, hidden), adjacency),
        54, flops=2 * limit * tile_rows * tile_rows * hidden, size=adjacency.size * 2, out_specs=(HBM, HBM),
    )
    plans = [Exchange(partitions, slots, step) for step in range(partitions.bit_length() - 1)]
    output, partial, message, keep = call(
        functools.partial(rest_kernel, partitions=partitions, slots=slots, columns=columns), "rest",
        [HBM] * 4 + [VMEM, HBM, HBM] + [VMEM] * 4 + [HBM],
        (
            struct((nodes, hidden), BF16),
            struct((nodes, inputs), F32),
            struct((plans[0].rows, inputs), BF16),
            struct((plans[0].keep, inputs), F32),
        ),
        [
            pltpu.VMEM((partitions * slots, inputs), F32),
            pltpu.VMEM((partitions * HUB_MOST, inputs), F32),
            pltpu.VMEM((nodes, hidden), BF16),
            pltpu.VMEM((dst_blocks, tile_rows, hidden), F32),
            pltpu.VMEM((dst_blocks, tile_rows, far_blocks * columns), BF16),
            pltpu.VMEM((far_blocks * columns, inputs), F32),
            pltpu.VMEM((far_blocks * columns, inputs), BF16),
            pltpu.VMEM((dst_blocks + 1, hidden, tile_rows), BF16),
            pltpu.VMEM((dst_blocks + 1, hidden, tile_rows), F32),
            pltpu.VMEM((far_blocks * columns, inputs), F32),
            pltpu.VMEM(adjacency.shape, BF16),
            lists,
            pltpu.SMEM((partitions,), jnp.int32),
            pltpu.SMEM((limit,), jnp.int32),
            pltpu.SMEM((limit,), jnp.int32),
            pltpu.SMEM((1,), jnp.int32),
            pltpu.SMEM((hubs,), jnp.int32),
            pltpu.SemaphoreType.DMA((limit,)),
            pltpu.SemaphoreType.DMA((3,)),
            pltpu.SemaphoreType.DMA((4,)),
        ],
        (
            tile_dst, tile_src, tile_count, owner,
            arrived, total, far, features, w_self, w_neigh, cotangent, adjacency,
        ),
        50, out_specs=(HBM, VMEM, VMEM, VMEM),
    )
    swap = [(0, 1), (1, 0)]
    tail = None
    for now, then in zip(plans, plans[1:]):
        got = lax.ppermute(message, "dom", [(q, q ^ now.half) for q in range(partitions)])
        if now is plans[0]:
            got, late_partial = lax.optimization_barrier((got, partial))
        outs = [struct((then.rows, inputs), BF16), struct((then.keep, inputs), F32)]
        if then is plans[-1]:
            outs.append(struct((then.rows - then.weights, inputs), BF16))
        message, keep, *tail = call(
            functools.partial(step_kernel, now=now, then=then), "step", [VMEM] * 3,
            tuple(outs), [], (message, got, keep), 16,
        )
    now = plans[-1]
    got = lax.ppermute(message, "dom", [(q, q ^ 1) for q in range(partitions)])
    cross = lax.ppermute(tail[0], ("dom", "feat"), [(k, k ^ 3) for k in range(2 * partitions)])
    other_keep = lax.ppermute(keep, "feat", swap)
    other_partial = lax.ppermute(late_partial, "feat", swap)
    summed, target = call(
        prepare_kernel, "prepare", [SMEM] * 4 + [VMEM] * 2,
        (struct((nodes, inputs), F32), struct((partitions * slots + HUB_MOST + 1,), jnp.int32)),
        [], (rows, counts, owner, hub_row, partial, other_partial), 16,
        flops=10**6, size=4 * 10**6, out_specs=(VMEM, SMEM),
    )
    grad_w_self, grad_w_neigh, grad_bias, grad_features = call(
        functools.partial(final_kernel, now=now), "final", [HBM] + [VMEM] * 6,
        (
            struct((inputs, hidden), F32), struct((inputs, hidden), F32), struct((1, hidden), F32),
            struct((nodes, inputs), BF16),
        ),
        [
            pltpu.VMEM((nodes + 8, inputs), F32),
            pltpu.SMEM((partitions * slots + HUB_MOST + 1,), jnp.int32),
            pltpu.SemaphoreType.DMA,
        ],
        (target, message, got, cross, keep, other_keep, summed), 32,
    )
    return (output, grad_features, grad_w_self, grad_w_neigh, grad_bias.reshape(hidden))


def solution(mesh):
    return jax.shard_map(
        local,
        mesh=mesh,
        in_specs=(
            P(("group", "dom"), None),
            P(None, "feat"),
            P(None, "feat"),
            P("feat"),
            P(("group", "dom"), "feat"),
            P(("group", "dom"), None, None),
            P(("group", "dom")),
            P(("group", "dom")),
            P(("group", "dom")),
            P(("group", "dom"), None, None),
            P(("group", "dom"), None),
            P("group", None),
            P("group"),
        ),
        out_specs=(
            P(("group", "dom"), "feat"),
            P(("group", "dom"), None),
            P("group", "feat"),
            P("group", "feat"),
            P(("group", "feat")),
        ),
        check_vma=False,
    )
```
